32 devices in a mesh: group: 2 (over x), sector: 16 (over z, y, core).
Axes of the slice: x: 2, y: 2, z: 4, core: 2. Of those that a mesh axis runs over, the one named last changes fastest.
Arguments:
- field: float32 [4, 5, 16, 16, 4096], P('group', None, None, 'sector'), parts along dimension 0, may hold values from -6 to 6
- axial_jac: float32 [2, 5, 5], replicated, may hold values from -2.5 to 2.5
- circ_jac: float32 [2, 5, 5], replicated, may hold values from -2.5 to 2.5
- left_char: float32 [2, 5, 5], replicated, may hold values from -2.5 to 2.5
- right_char: float32 [2, 5, 5], replicated, may hold values from -2.5 to 2.5
- mode_source: int32 [2, 256], replicated, may hold values from 0 to 255, as said below
- mode_target: int32 [2, 256], replicated, may hold values from 0 to 255, as said below
- mode_count: int32 [2], replicated, may hold values from 128 to 256, as said below
- section_offset: int32 [4], replicated, may hold values from 0 to 511
Outputs:
- advanced: float32 [4, 5, 16, 16, 4096], P('group', None, None, 'sector'), parts along dimension 0
The draws below stay inside these ranges and needn't reach their ends.
There are 2 independent parts, one for each index of `group`. The reference program is written for one: setup_inputs(seed, part) draws one part's arguments, and reference() takes and returns one part's arrays. A program takes and returns all parts, laid end to end along the dimension named above; an argument that names none is the same for every part. Nothing has to cross between parts.
Inputs may be any that keep to these rules, and one draw needn't show every extreme that they name: `mode_source`: each row is a permutation of 0 to 255; entries at pair index mode_count[d] or beyond are padding. `mode_target`: each row is a permutation of 0 to 255; entries at pair index mode_count[d] or beyond are padding. `mode_count`: the first direction's count is 256.
All inputs are finite; a program needn't handle non-finite values.
Results may differ from the reference program's by a relative error of at most 0.00005.
Values sent between devices are 32-bit elements; how exact they have to be, the bound alone decides.
A program may use at most 128 MiB of HBM per device.

```python
import math
import jax
import jax.numpy as jnp
from jax import lax

NTH = 512
VARS = 5
NB = 8
NR = 128
AX = 16
K = 256
CELLS = 4096
N_SECTOR = 16


def draw_mode_source(key, part):
    key = jax.random.fold_in(key, 11)
    return jnp.stack([jax.random.permutation(jax.random.fold_in(key, 1), K), jax.random.permutation(jax.random.fold_in(key, 2), K)]).astype(jnp.int32)


def draw_mode_target(key, part):
    key = jax.random.fold_in(key, 23)
    return jnp.stack([jax.random.permutation(jax.random.fold_in(key, 1), K), jax.random.permutation(jax.random.fold_in(key, 2), K)]).astype(jnp.int32)


def draw_mode_count(key, part):
    key = jax.random.fold_in(key, 37)
    second = jax.random.randint(key, (1,), K // 2, K + 1)
    return jnp.concatenate([jnp.full((1,), K, jnp.int32), second.astype(jnp.int32)])


def set_ends(values, stream_key, low, largest):
    shape = values.shape
    place = [jax.random.randint(jax.random.fold_in(stream_key, axis), (), 0, shape[axis]) for axis in range(len(shape))]
    values = values.at[tuple(place)].set(low)
    longest = shape.index(max(shape))
    place[longest] = (place[longest] + 1) % shape[longest]
    return values.at[tuple(place)].set(largest)


def level_of(key, shape, shards, low, high):
    factor_of, own = 1.0, jax.random.fold_in(key, 6)
    for position, blocks in shards:
        heights = jnp.exp(jax.random.uniform(jax.random.fold_in(own, position), (blocks,), jnp.float32, low / len(shards), high / len(shards)))
        factor_of = factor_of * jnp.repeat(heights, shape[position] // blocks).reshape([-1 if axis == position else 1 for axis in range(len(shape))])
    return factor_of


def bell_draw(rng, extent, spread, bound, shards=(), kind=jnp.bfloat16):
    values = jax.random.normal(rng, extent, jnp.float32) * spread
    if len(shards) > 0:
        values = level_of(rng, extent, shards, -0.22, 0.18) * values
    return jnp.clip(values, min=-bound, max=bound).astype(kind)


def setup_inputs(seed: int = 0, part: int = 0) -> dict:
    key_of = jax.random.split(jax.random.key(seed), 10)
    own_keys = jax.random.split(jax.random.fold_in(key_of[9], part), 10)
    field = bell_draw(own_keys[0], (2, VARS, AX, N_SECTOR, CELLS), 1.0, 6.0, ((3, 16),), jnp.float32)
    axial_jac = bell_draw(key_of[1], (2, VARS, VARS), VARS ** -0.5, 2.5, (), jnp.float32)
    circ_jac = bell_draw(key_of[2], (2, VARS, VARS), VARS ** -0.5, 2.5, (), jnp.float32)
    left_char = bell_draw(key_of[3], (2, VARS, VARS), VARS ** -0.5, 2.5, (), jnp.float32)
    right_char = bell_draw(key_of[4], (2, VARS, VARS), VARS ** -0.5, 2.5, (), jnp.float32)
    mode_source = draw_mode_source(jax.random.fold_in(key_of[9], 71), part)
    mode_target = draw_mode_target(jax.random.fold_in(key_of[9], 71), part)
    mode_count = draw_mode_count(jax.random.fold_in(key_of[9], 71), part)
    section_offset = set_ends(jax.random.randint(key_of[8], (4,), 0, NTH), jax.random.fold_in(key_of[8], 1), 0, NTH - 1).astype(jnp.int32)
    return {"field": field, "axial_jac": axial_jac, "circ_jac": circ_jac, "left_char": left_char, "right_char": right_char, "mode_source": mode_source, "mode_target": mode_target, "mode_count": mode_count, "section_offset": section_offset}


precise = lax.Precision.HIGHEST
time_step = 0.2
diffusion = 0.05


def fourier_tables():
    theta = jnp.arange(NTH, dtype=jnp.int32)
    modes = jnp.arange(K, dtype=jnp.int32)
    phase = ((theta[:, None] * modes[None, :]) % NTH).astype(jnp.float32) * (2.0 * math.pi / NTH)
    cosine = jnp.cos(phase)
    sine = jnp.sin(phase)
    forward = jnp.concatenate([cosine, -sine], axis=1)
    weights = jnp.where(modes == 0, 1.0 / NTH, 2.0 / NTH).astype(jnp.float32)
    inverse = jnp.concatenate([(cosine * weights[None, :]).T, -(sine * weights[None, :]).T], axis=0)
    return forward, inverse


def matching(source, target, count, offset, sign):
    modes = jnp.arange(K, dtype=jnp.int32)
    valid = (modes < count).astype(jnp.float32)
    phase = ((source * offset) % NTH).astype(jnp.float32) * (sign * 2.0 * math.pi / NTH)
    weighted_cos = jnp.cos(phase) * valid
    weighted_sin = jnp.sin(phase) * valid
    one_source = (source[:, None] == modes[None, :]).astype(jnp.float32)
    one_target = (target[:, None] == modes[None, :]).astype(jnp.float32)
    keep = jnp.dot(one_source.T, weighted_cos[:, None] * one_target, precision=precise)
    turn = jnp.dot(one_source.T, weighted_sin[:, None] * one_target, precision=precise)
    return jnp.concatenate([jnp.concatenate([keep, turn], 1), jnp.concatenate([-turn, keep], 1)], 0)


def transform(planes, left_char, right_char, mats, forward, inverse):
    spectrum = jnp.einsum('dvrt,tk->dvrk', planes, forward, precision=precise)
    charac = jnp.einsum('dwv,dvrk->dwrk', left_char, spectrum, precision=precise)
    moved = jnp.einsum('dwrk,dkm->dwrm', charac, mats, precision=precise)
    back = jnp.einsum('dvw,dwrm->dvrm', right_char, moved, precision=precise)
    return jnp.einsum('dvrm,mt->dvrt', back, inverse, precision=precise)


def stencil(state, cycle, ghosts, axial_jac, circ_jac):
    zero = jnp.zeros_like(ghosts[0])
    lower = jnp.stack([zero, ghosts[0]])
    upper = jnp.stack([ghosts[1], zero])
    axial = jnp.concatenate([lower[:, :, None], state, upper[:, :, None]], axis=2)
    radial = jnp.pad(state, ((0, 0), (0, 0), (0, 0), (0, 0), (1, 1)))
    d_axial = (axial[:, :, 2:] - axial[:, :, :-2]) * 0.5
    d_circ = (cycle[:, :, :, 2:] - cycle[:, :, :, :-2]) * 0.5
    neighbours = axial[:, :, 2:] + axial[:, :, :-2] + cycle[:, :, :, 2:] + cycle[:, :, :, :-2]
    neighbours = neighbours + radial[..., 2:] + radial[..., :-2]
    flux = jnp.einsum('rvw,rwatn->rvatn', axial_jac, d_axial, precision=precise)
    flux = flux + jnp.einsum('rvw,rwatn->rvatn', circ_jac, d_circ, precision=precise)
    return -flux + diffusion * (neighbours - 6.0 * state)


def to_grid(bricks):
    sectors = N_SECTOR // NB
    slots = NTH // sectors
    rows = NR // NB
    depth = bricks.shape[2]
    ordered = jnp.roll(bricks, NB // 2, axis=3)
    split = ordered.reshape(2, VARS, depth, sectors, NB, slots, rows)
    return jnp.transpose(split, (0, 1, 2, 3, 5, 4, 6)).reshape(2, VARS, depth, NTH, NR)


def from_grid(grid):
    sectors = N_SECTOR // NB
    slots = NTH // sectors
    rows = NR // NB
    depth = grid.shape[2]
    split = grid.reshape(2, VARS, depth, sectors, slots, NB, rows)
    ordered = jnp.transpose(split, (0, 1, 2, 3, 5, 4, 6)).reshape(2, VARS, depth, N_SECTOR, slots * rows)
    return jnp.roll(ordered, -(NB // 2), axis=3)


def reference(field, axial_jac, circ_jac, left_char, right_char, mode_source, mode_target, mode_count, section_offset):
    forward, inverse = fourier_tables()
    grid = to_grid(field)

    def rates(state, offset):
        mats = jnp.stack([matching(mode_source[0], mode_target[0], mode_count[0], offset, 1.0),
                          matching(mode_source[1], mode_target[1], mode_count[1], offset, -1.0)])
        planes = jnp.transpose(jnp.stack([state[0, :, -1], state[1, :, 0]]), (0, 1, 3, 2))
        ghosts = transform(planes, left_char, right_char, mats, forward, inverse)
        ghosts = jnp.transpose(ghosts, (0, 1, 3, 2))
        cycle = jnp.concatenate([state[:, :, :, -1:], state, state[:, :, :, :1]], axis=3)
        return stencil(state, cycle, ghosts, axial_jac, circ_jac)

    first = rates(grid, section_offset[0])
    second = rates(grid + (0.5 * time_step) * first, section_offset[1])
    third = rates(grid + (0.5 * time_step) * second, section_offset[2])
    fourth = rates(grid + time_step * third, section_offset[3])
    result = grid + (time_step / 6.0) * (first + 2.0 * second + 2.0 * third + fourth)
    return from_grid(result)
```

```python
import functools
import math

import jax
import jax.numpy as jnp
import numpy as np
from jax import lax
from jax.experimental import pallas as pl
from jax.experimental.pallas import tpu as pltpu
from jax.sharding import PartitionSpec as P

NTH = 512
VARS = 5
NB = 8
NR = 128
K = 256


precise = lax.Precision.HIGHEST
time_step = 0.2
diffusion = 0.05


def passed_along(block, axis, distance):
    devices = range(lax.axis_size(axis))
    route = [((i - distance) % len(devices), i) for i in devices]
    return lax.ppermute(block, axis, route)


def with_halo(x, sides, width):
    for axis, dim in sides:
        size, length = (lax.axis_size(axis), x.shape[dim])
        up = [(i, (i + 1) % size) for i in range(size)]
        down = [(j, i) for i, j in up]
        last = lax.slice_in_dim(x, length - width, length, axis=dim)
        first = lax.slice_in_dim(x, 0, width, axis=dim)
        before = lax.ppermute(last, axis, up)
        after = lax.ppermute(first, axis, down)
        x = jnp.concatenate([before, x, after], axis=dim)
    return x


def fourier_tables():
    theta = jnp.arange(NTH, dtype=jnp.int32)
    modes = jnp.arange(K, dtype=jnp.int32)
    phase = (theta[:, None] * modes[None, :] % NTH).astype(jnp.float32) * (2.0 * math.pi / NTH)
    cosine = jnp.cos(phase)
    sine = jnp.sin(phase)
    forward = jnp.concatenate([cosine, -sine], axis=1)
    weights = jnp.where(modes == 0, 1.0 / NTH, 2.0 / NTH).astype(jnp.float32)
    inverse = jnp.concatenate([(cosine * weights[None, :]).T, -(sine * weights[None, :]).T], axis=0)
    return (forward, inverse)


def matching(source, target, count, offset, sign):
    modes = jnp.arange(K, dtype=jnp.int32)
    valid = (modes < count).astype(jnp.float32)
    phase = (source * offset % NTH).astype(jnp.float32) * (sign * 2.0 * math.pi / NTH)
    weighted_cos = jnp.cos(phase) * valid
    weighted_sin = jnp.sin(phase) * valid
    one_source = (source[:, None] == modes[None, :]).astype(jnp.float32)
    one_target = (target[:, None] == modes[None, :]).astype(jnp.float32)
    keep = jnp.dot(one_source.T, weighted_cos[:, None] * one_target, precision=precise)
    turn = jnp.dot(one_source.T, weighted_sin[:, None] * one_target, precision=precise)
    return jnp.concatenate([jnp.concatenate([keep, turn], 1), jnp.concatenate([-turn, keep], 1)], 0)


def transform(planes, left_char, right_char, mats, forward, inverse):
    spectrum = jnp.einsum("dvrt,tk->dvrk", planes, forward, precision=precise)
    charac = jnp.einsum("dwv,dvrk->dwrk", left_char, spectrum, precision=precise)
    moved = jnp.einsum("dwrk,dkm->dwrm", charac, mats, precision=precise)
    back = jnp.einsum("dvw,dwrm->dvrm", right_char, moved, precision=precise)
    return jnp.einsum("dvrm,mt->dvrt", back, inverse, precision=precise)


def stencil(state, cycle, radial, ghosts, axial_jac, circ_jac):
    zero = jnp.zeros_like(ghosts[0])
    lower = jnp.stack([zero, ghosts[0]])
    upper = jnp.stack([ghosts[1], zero])
    axial = jnp.concatenate([lower[:, :, None], state, upper[:, :, None]], axis=2)
    d_axial = (axial[:, :, 2:] - axial[:, :, :-2]) * 0.5
    d_circ = (cycle[:, :, :, 2:] - cycle[:, :, :, :-2]) * 0.5
    neighbours = axial[:, :, 2:] + axial[:, :, :-2] + cycle[:, :, :, 2:] + cycle[:, :, :, :-2]
    neighbours = neighbours + radial[..., 2:] + radial[..., :-2]
    flux = jnp.einsum("rvw,rwatn->rvatn", axial_jac, d_axial, precision=precise)
    flux = flux + jnp.einsum("rvw,rwatn->rvatn", circ_jac, d_circ, precision=precise)
    return -flux + diffusion * (neighbours - 6.0 * state)


def general_path(
    field,
    axial_jac,
    circ_jac,
    left_char,
    right_char,
    mode_source,
    mode_target,
    mode_count,
    section_offset,
):
    forward, inverse = fourier_tables()
    devices = lax.axis_size("sector")
    index = lax.axis_index("sector")
    depth = field.shape[2]
    rows = NR // NB
    slots = field.shape[4] // rows
    sectors = devices // NB
    per_band = devices // NB
    owned = NR // devices
    half_band = NB // 2
    position = (index + half_band) % devices
    band = position % NB
    cell_band = index // per_band
    low_keep = (band > 0).astype(jnp.float32)
    high_keep = (band < NB - 1).astype(jnp.float32)
    grid = field.reshape(2, VARS, depth, slots, rows)

    def rates(state, offset):
        mats = jnp.stack(
            [
                matching(mode_source[0], mode_target[0], mode_count[0], offset, 1.0),
                matching(mode_source[1], mode_target[1], mode_count[1], offset, -1.0),
            ]
        )
        planes = jnp.stack([state[0, :, -1], state[1, :, 0]])
        outgoing = jnp.transpose(planes.reshape(2, VARS, slots, per_band, owned), (3, 0, 1, 2, 4))
        buffer = jnp.zeros((devices, 2, VARS, slots, owned), jnp.float32)
        buffer = lax.dynamic_update_slice_in_dim(buffer, outgoing, band * per_band, 0)
        arrived = lax.all_to_all(buffer, "sector", split_axis=0, concat_axis=0, tiled=True)
        arrived = jnp.roll(arrived, half_band, axis=0).reshape(sectors, NB, 2, VARS, slots, owned)
        picked = lax.dynamic_index_in_dim(arrived, cell_band, 1, keepdims=False)
        banded = jnp.transpose(picked, (1, 2, 4, 0, 3)).reshape(2, VARS, owned, sectors * slots)
        band_ghosts = transform(banded, left_char, right_char, mats, forward, inverse)
        reply = jnp.transpose(band_ghosts.reshape(2, VARS, owned, sectors, slots), (3, 0, 1, 4, 2))
        back = jnp.zeros((sectors, NB, 2, VARS, slots, owned), jnp.float32)
        back = lax.dynamic_update_index_in_dim(back, reply, cell_band, 1)
        back = jnp.roll(back.reshape(devices, 2, VARS, slots, owned), -half_band, axis=0)
        returned = lax.all_to_all(back, "sector", split_axis=0, concat_axis=0, tiled=True)
        mine = lax.dynamic_slice_in_dim(returned, band * per_band, per_band, 0)
        ghosts = jnp.transpose(mine, (1, 2, 3, 0, 4)).reshape(2, VARS, slots, rows)
        before = passed_along(state[:, :, :, -1:], "sector", NB)
        after = passed_along(state[:, :, :, :1], "sector", -NB)
        cycle = jnp.concatenate([before, state, after], axis=3)
        widened = with_halo(state, (("sector", 4),), 1)
        radial = jnp.concatenate(
            [widened[..., :1] * low_keep, widened[..., 1:-1], widened[..., -1:] * high_keep], axis=4
        )
        return stencil(state, cycle, radial, ghosts, axial_jac, circ_jac)

    first = rates(grid, section_offset[0])
    second = rates(grid + 0.5 * time_step * first, section_offset[1])
    third = rates(grid + 0.5 * time_step * second, section_offset[2])
    fourth = rates(grid + time_step * third, section_offset[3])
    result = grid + time_step / 6.0 * (first + 2.0 * second + 2.0 * third + fourth)
    return result.reshape(field.shape)


ROWS = 32
LANES = 128
RADIAL = 16
PER_ROW = LANES // RADIAL
HALF = ROWS * PER_ROW
STATE_STEP = (0.5 * time_step, 0.5 * time_step, time_step)
SUM_STEP = (time_step / 6.0, time_step / 3.0, time_step / 3.0, time_step / 6.0)


def split(x):
    high = x.astype(jnp.bfloat16)
    return high, (x - high.astype(jnp.float32)).astype(jnp.bfloat16)


def split_tables():
    point = np.arange(2 * HALF).reshape(2, ROWS, PER_ROW).transpose(0, 2, 1).reshape(2, HALF)
    modes = np.arange(K)
    phase = 2.0 * np.pi * ((point[:, :, None] * modes) % NTH) / NTH
    weights = np.where(modes == 0, 1.0 / NTH, 2.0 / NTH)
    forward = np.concatenate([np.cos(phase), -np.sin(phase)], axis=2).transpose(0, 2, 1)
    inverse = np.concatenate([weights * np.cos(phase), -weights * np.sin(phase)], axis=2)

    def both(x):
        high = x.astype(jnp.bfloat16)
        low = (x - high.astype(np.float64)).astype(jnp.bfloat16)
        return np.stack([high, low], axis=1)

    return both(forward), both(inverse)


def dot3(a_high, a_low, b):
    b_high, b_low = split(b)
    dot = functools.partial(jnp.dot, preferred_element_type=jnp.float32)
    return dot(a_high, b_high) + (dot(a_high, b_low) + dot(a_low, b_high))


def turned(x, shift, axis=1):
    if isinstance(shift, int):
        shift = shift % x.shape[axis]
        return x if shift == 0 else pltpu.roll(x, shift, axis)
    return pltpu.roll(x, lax.rem(shift + 2 * LANES, LANES), axis)


def packed(planes):
    group = lax.broadcasted_iota(jnp.int32, (ROWS, LANES), 1) // RADIAL
    parts = []
    for c in range(PER_ROW):
        part = jnp.zeros((ROWS, LANES), jnp.float32)
        for v in range(VARS):
            part = jnp.where(group == v, turned(planes[v], RADIAL * (v - c)), part)
        parts.append(part)
    return jnp.concatenate(parts, axis=0)


def unpacked(x, v):
    group = lax.broadcasted_iota(jnp.int32, (ROWS, LANES), 1) // RADIAL
    plane = turned(x[:ROWS], -RADIAL * v)
    for c in range(1, PER_ROW):
        piece = turned(x[c * ROWS:(c + 1) * ROWS], RADIAL * (c - v))
        plane = jnp.where(group == c, piece, plane)
    return plane


def step_kernel(
    field, axial_jac, circ_jac, left_char, right_char, count, offset,
    source, target, forward, inverse, out,
    state, seam_in, radial_out, radial_in, circ_out, circ_in,
    gather, phases, ghost_map, spectrum,
    seam_send, seam_recv, radial_send, radial_recv, circ_send, circ_recv,
):
    depth = field.shape[2]
    devices = 2 * NB
    me = lax.axis_index("sector")
    position = lax.rem(me + NB // 2, devices)
    sector = position // NB
    band = lax.rem(position, NB)
    right = lax.rem(me + 1, devices)
    left = lax.rem(me + devices - 1, devices)
    partner = lax.rem(me + NB, devices)
    low_keep = (band > 0).astype(jnp.float32)
    high_keep = (band < NB - 1).astype(jnp.float32)

    barrier = pltpu.get_barrier_semaphore()
    for other in (left, right, partner):
        pl.semaphore_signal(
            barrier, inc=1, device_id={"sector": other}, device_id_type=pl.DeviceIdType.MESH
        )

    lane = lax.broadcasted_iota(jnp.int32, (ROWS, LANES), 1)
    row = lax.broadcasted_iota(jnp.int32, (ROWS, LANES), 0)
    radial = lane % RADIAL
    lane1 = lax.broadcasted_iota(jnp.int32, (1, LANES), 1)
    group1 = lane1 // RADIAL

    def pack(slot, r, a, new):
        last = jnp.zeros((1, LANES), jnp.float32)
        first = jnp.zeros((1, LANES), jnp.float32)
        here = radial == a
        for v in range(VARS):
            n = new[v]
            radial_out[slot, 0, r, v] = jnp.where(
                here, turned(n, a - (RADIAL - 1)), radial_out[slot, 0, r, v]
            )
            radial_out[slot, 1, r, v] = jnp.where(here, turned(n, a), radial_out[slot, 1, r, v])
            last = jnp.where(group1 == v, turned(n[ROWS - 1:], RADIAL * (v + 1)), last)
            first = jnp.where(group1 == v, turned(n[:1], RADIAL * v), first)
        circ_out[slot, 0, r, pl.ds(a, 1), :] = last
        circ_out[slot, 1, r, pl.ds(a, 1), :] = first

    def take_in(i, carry):
        r, a = i // depth, lax.rem(i, depth)
        new = [field[r, v, a] for v in range(VARS)]
        for v in range(VARS):
            state[0, r, v, a + 1] = new[v]
        pack(0, r, a, new)
        return carry

    lax.fori_loop(0, 2 * depth, take_in, 0)
    for slot in range(2):
        for v in range(VARS):
            state[slot, 0, v, 0] = jnp.zeros((ROWS, LANES), jnp.float32)
            state[slot, 1, v, depth + 1] = jnp.zeros((ROWS, LANES), jnp.float32)

    pl.semaphore_wait(barrier, 3)

    def remote(src, dst, send, recv, device):
        return pltpu.make_async_remote_copy(
            src_ref=src, dst_ref=dst, send_sem=send, recv_sem=recv,
            device_id={"sector": device}, device_id_type=pl.DeviceIdType.MESH,
        )

    def copies(k, cur):
        seams = [
            remote(
                state.at[cur, d, :, depth if d == 0 else 1], seam_in.at[k, d],
                seam_send.at[k, d], seam_recv.at[k, d], partner,
            )
            for d in range(2)
        ]
        sides = [
            remote(
                radial_out.at[k, d], radial_in.at[k, d],
                radial_send.at[k, d], radial_recv.at[k, d], right if d == 0 else left,
            )
            for d in range(2)
        ]
        circ = remote(circ_out.at[k], circ_in.at[k], circ_send.at[k], circ_recv.at[k], partner)
        return seams, sides, circ

    def tables():
        wide = lax.broadcasted_iota(jnp.int32, (K, K), 0)
        pair = lax.broadcasted_iota(jnp.int32, (K, K), 1)
        for d in range(2):
            from_source = (source[d:d + 1, :] == wide).astype(jnp.float32).astype(jnp.bfloat16)
            to_target = jnp.where(
                (target[d:d + 1, :] == wide) & (pair < count[d]), 1.0, 0.0
            ).astype(jnp.bfloat16)
            moves = lax.dot_general(
                to_target, from_source, (((1,), (1,)), ((), ())),
                preferred_element_type=jnp.float32,
            ).astype(jnp.bfloat16)
            for part in range(2):
                for wave in range(2):
                    gather[d, part, :, wave * K:(wave + 1) * K] = jnp.dot(
                        inverse[sector, part, :, wave * K:(wave + 1) * K], moves,
                        preferred_element_type=jnp.float32,
                    ).astype(jnp.bfloat16)
            for v in range(VARS):
                for w in range(VARS):
                    total = right_char[d, v, 0] * left_char[d, 0, w]
                    for c in range(1, VARS):
                        total = total + right_char[d, v, c] * left_char[d, c, w]
                    ghost_map[d, v * VARS + w] = total
        mode = lax.broadcasted_iota(jnp.int32, (K, LANES), 0)
        for s in range(4):
            angle = ((mode * offset[s]) & (NTH - 1)).astype(jnp.float32) * (2.0 * math.pi / NTH)
            phases[s, 0] = jnp.cos(angle)
            phases[s, 1] = jnp.sin(angle)

    def own_spectrum(cur):
        both = jnp.concatenate(
            [
                packed([state[cur, 0, v, depth] for v in range(VARS)]),
                packed([state[cur, 1, v, 1] for v in range(VARS)]),
            ],
            axis=1,
        )
        spectrum[...] = dot3(forward[sector, 0], forward[sector, 1], both)

    def make_ghosts(k, cur):
        both = jnp.concatenate(
            [packed([seam_in[k, d, v] for v in range(VARS)]) for d in range(2)], axis=1
        )
        whole = spectrum[...] + dot3(forward[1 - sector, 0], forward[1 - sector, 1], both)
        cosine, sine = phases[k, 0], phases[k, 1]
        for d in range(2):
            even = whole[:K, d * LANES:(d + 1) * LANES]
            odd = whole[K:, d * LANES:(d + 1) * LANES]
            turn = sine if d == 0 else -sine
            moved = jnp.concatenate([cosine * even - turn * odd, turn * even + cosine * odd], axis=0)
            raw = dot3(gather[d, 0], gather[d, 1], moved)
            planes = [unpacked(raw, w) for w in range(VARS)]
            for v in range(VARS):
                ghost = ghost_map[d, v * VARS] * planes[0]
                for w in range(1, VARS):
                    ghost = ghost + ghost_map[d, v * VARS + w] * planes[w]
                if d == 0:
                    state[cur, 1, v, 0] = ghost
                else:
                    state[cur, 0, v, depth + 1] = ghost

    def advance(k, cur, r, a, first, last):
        up_row = circ_in[k, 0, r, pl.ds(a, 1), :]
        down_row = circ_in[k, 1, r, pl.ds(a, 1), :]
        along, around, spread = [], [], []
        for w in range(VARS):
            x = state[cur, r, w, a + 1]
            before, after = state[cur, r, w, a], state[cur, r, w, a + 2]
            up = jnp.where(row == 0, turned(up_row, LANES - RADIAL - RADIAL * w), turned(x, 1, 0))
            down = jnp.where(row == ROWS - 1, turned(down_row, -RADIAL * w), turned(x, -1, 0))
            previous = turned(jnp.where(lane >= LANES - RADIAL, up, x), RADIAL)
            following = turned(jnp.where(lane < RADIAL, down, x), -RADIAL)
            inner = jnp.where(
                radial == 0, turned(radial_in[k, 0, r, w], -a) * low_keep, turned(x, 1)
            )
            outer = jnp.where(
                radial == RADIAL - 1,
                turned(radial_in[k, 1, r, w], RADIAL - 1 - a) * high_keep,
                turned(x, -1),
            )
            along.append(after - before)
            around.append(following - previous)
            spread.append(
                diffusion * ((after + before) + (following + previous) + (inner + outer) - 6.0 * x)
            )
        if last:
            state_step, sum_step = None, SUM_STEP[3]
        else:
            state_step = jnp.where(k == 2, STATE_STEP[2], STATE_STEP[0])
            sum_step = jnp.where(k == 0, SUM_STEP[0], SUM_STEP[1])
        new = []
        for v in range(VARS):
            rate = spread[v]
            for w in range(VARS):
                rate = rate - (0.5 * axial_jac[r, v, w]) * along[w]
                rate = rate - (0.5 * circ_jac[r, v, w]) * around[w]
            if last:
                out[r, v, a] = out[r, v, a] + sum_step * rate
            else:
                base = field[r, v, a]
                total = jnp.where(k == 0, base, out[r, v, a])
                out[r, v, a] = total + sum_step * rate
                n = base + state_step * rate
                state[1 - cur, r, v, a + 1] = n
                new.append(n)
        if not last:
            pack(k + 1, r, a, new)

    def stage(k, first=False, last=False):
        cur = lax.rem(k, 2) if not isinstance(k, int) else k % 2
        seams, sides, circ = copies(k, cur)
        for copy in seams + sides + [circ]:
            copy.start()
        own_spectrum(cur)
        for copy in sides + [circ]:
            copy.wait_recv()

        def inside(i, carry):
            r = i // (depth - 1)
            advance(k, cur, r, lax.rem(i, depth - 1) + r, first, last)
            return carry

        lax.fori_loop(0, 2 * (depth - 1), inside, 0)
        for copy in seams:
            copy.wait_recv()
        make_ghosts(k, cur)

        def edge(r, carry):
            advance(k, cur, r, (depth - 1) * (1 - r), first, last)
            return carry

        lax.fori_loop(0, 2, edge, 0)
        for copy in seams + sides + [circ]:
            copy.wait_send()

    tables()

    def early(k, carry):
        stage(k)
        return carry

    lax.fori_loop(0, 3, early, 0)
    stage(3, last=True)


def fast_path(
    field, axial_jac, circ_jac, left_char, right_char, mode_source, mode_target, mode_count,
    section_offset,
):
    depth = field.shape[2]
    grid = field.reshape(2, VARS, depth, ROWS, LANES)
    forward, inverse = split_tables()
    smem = pl.BlockSpec(memory_space=pltpu.SMEM)
    vmem = pl.BlockSpec(memory_space=pltpu.VMEM)
    plane = (ROWS, LANES)
    result = pl.pallas_call(
        step_kernel,
        out_shape=jax.ShapeDtypeStruct(grid.shape, jnp.float32),
        in_specs=[vmem] + [smem] * 6 + [vmem] * 4,
        out_specs=vmem,
        scratch_shapes=[
            pltpu.VMEM((2, 2, VARS, depth + 2) + plane, jnp.float32),
            pltpu.VMEM((4, 2, VARS) + plane, jnp.float32),
            pltpu.VMEM((4, 2, 2, VARS) + plane, jnp.float32),
            pltpu.VMEM((4, 2, 2, VARS) + plane, jnp.float32),
            pltpu.VMEM((4, 2, 2, depth, LANES), jnp.float32),
            pltpu.VMEM((4, 2, 2, depth, LANES), jnp.float32),
            pltpu.VMEM((2, 2, HALF, 2 * K), jnp.bfloat16),
            pltpu.VMEM((4, 2, K, LANES), jnp.float32),
            pltpu.SMEM((2, VARS * VARS), jnp.float32),
            pltpu.VMEM((2 * K, 2 * LANES), jnp.float32),
            pltpu.SemaphoreType.DMA((4, 2)),
            pltpu.SemaphoreType.DMA((4, 2)),
            pltpu.SemaphoreType.DMA((4, 2)),
            pltpu.SemaphoreType.DMA((4, 2)),
            pltpu.SemaphoreType.DMA((4,)),
            pltpu.SemaphoreType.DMA((4,)),
        ],
        compiler_params=pltpu.CompilerParams(
            collective_id=0, has_side_effects=True, vmem_limit_bytes=48 * 1024 * 1024
        ),
    )(
        grid, axial_jac, circ_jac, left_char, right_char, mode_count, section_offset,
        mode_source, mode_target, jnp.asarray(forward), jnp.asarray(inverse),
    )
    return result.reshape(field.shape)


def on_device(field, *rest):
    fits = lax.axis_size("sector") == 2 * NB and field.shape[4] == ROWS * LANES
    return (fast_path if fits else general_path)(field, *rest)


def solution(mesh):
    in_specs = (P("group", None, None, "sector", None), P(), P(), P(), P(), P(), P(), P(), P())
    out_specs = P("group", None, None, "sector", None)
    return jax.shard_map(
        on_device, mesh=mesh, in_specs=in_specs, out_specs=out_specs, check_vma=False
    )
```

```python
import functools
import math

import jax
import jax.numpy as jnp
import numpy as np
from jax import lax
from jax.experimental import pallas as pl
from jax.experimental.pallas import tpu as pltpu
from jax.sharding import PartitionSpec as P

NTH = 512
VARS = 5
NB = 8
NR = 128
K = 256


precise = lax.Precision.HIGHEST
time_step = 0.2
diffusion = 0.05


def passed_along(block, axis, distance):
    devices = range(lax.axis_size(axis))
    route = [((i - distance) % len(devices), i) for i in devices]
    return lax.ppermute(block, axis, route)


def with_halo(x, sides, width):
    for axis, dim in sides:
        size, length = (lax.axis_size(axis), x.shape[dim])
        up = [(i, (i + 1) % size) for i in range(size)]
        down = [(j, i) for i, j in up]
        last = lax.slice_in_dim(x, length - width, length, axis=dim)
        first = lax.slice_in_dim(x, 0, width, axis=dim)
        before = lax.ppermute(last, axis, up)
        after = lax.ppermute(first, axis, down)
        x = jnp.concatenate([before, x, after], axis=dim)
    return x


def fourier_tables():
    theta = jnp.arange(NTH, dtype=jnp.int32)
    modes = jnp.arange(K, dtype=jnp.int32)
    phase = (theta[:, None] * modes[None, :] % NTH).astype(jnp.float32) * (2.0 * math.pi / NTH)
    cosine = jnp.cos(phase)
    sine = jnp.sin(phase)
    forward = jnp.concatenate([cosine, -sine], axis=1)
    weights = jnp.where(modes == 0, 1.0 / NTH, 2.0 / NTH).astype(jnp.float32)
    inverse = jnp.concatenate([(cosine * weights[None, :]).T, -(sine * weights[None, :]).T], axis=0)
    return (forward, inverse)


def matching(source, target, count, offset, sign):
    modes = jnp.arange(K, dtype=jnp.int32)
    valid = (modes < count).astype(jnp.float32)
    phase = (source * offset % NTH).astype(jnp.float32) * (sign * 2.0 * math.pi / NTH)
    weighted_cos = jnp.cos(phase) * valid
    weighted_sin = jnp.sin(phase) * valid
    one_source = (source[:, None] == modes[None, :]).astype(jnp.float32)
    one_target = (target[:, None] == modes[None, :]).astype(jnp.float32)
    keep = jnp.dot(one_source.T, weighted_cos[:, None] * one_target, precision=precise)
    turn = jnp.dot(one_source.T, weighted_sin[:, None] * one_target, precision=precise)
    return jnp.concatenate([jnp.concatenate([keep, turn], 1), jnp.concatenate([-turn, keep], 1)], 0)


def transform(planes, left_char, right_char, mats, forward, inverse):
    spectrum = jnp.einsum("dvrt,tk->dvrk", planes, forward, precision=precise)
    charac = jnp.einsum("dwv,dvrk->dwrk", left_char, spectrum, precision=precise)
    moved = jnp.einsum("dwrk,dkm->dwrm", charac, mats, precision=precise)
    back = jnp.einsum("dvw,dwrm->dvrm", right_char, moved, precision=precise)
    return jnp.einsum("dvrm,mt->dvrt", back, inverse, precision=precise)


def stencil(state, cycle, radial, ghosts, axial_jac, circ_jac):
    zero = jnp.zeros_like(ghosts[0])
    lower = jnp.stack([zero, ghosts[0]])
    upper = jnp.stack([ghosts[1], zero])
    axial = jnp.concatenate([lower[:, :, None], state, upper[:, :, None]], axis=2)
    d_axial = (axial[:, :, 2:] - axial[:, :, :-2]) * 0.5
    d_circ = (cycle[:, :, :, 2:] - cycle[:, :, :, :-2]) * 0.5
    neighbours = axial[:, :, 2:] + axial[:, :, :-2] + cycle[:, :, :, 2:] + cycle[:, :, :, :-2]
    neighbours = neighbours + radial[..., 2:] + radial[..., :-2]
    flux = jnp.einsum("rvw,rwatn->rvatn", axial_jac, d_axial, precision=precise)
    flux = flux + jnp.einsum("rvw,rwatn->rvatn", circ_jac, d_circ, precision=precise)
    return -flux + diffusion * (neighbours - 6.0 * state)


def general_path(
    field,
    axial_jac,
    circ_jac,
    left_char,
    right_char,
    mode_source,
    mode_target,
    mode_count,
    section_offset,
):
    forward, inverse = fourier_tables()
    devices = lax.axis_size("sector")
    index = lax.axis_index("sector")
    depth = field.shape[2]
    rows = NR // NB
    slots = field.shape[4] // rows
    sectors = devices // NB
    per_band = devices // NB
    owned = NR // devices
    half_band = NB // 2
    position = (index + half_band) % devices
    band = position % NB
    cell_band = index // per_band
    low_keep = (band > 0).astype(jnp.float32)
    high_keep = (band < NB - 1).astype(jnp.float32)
    grid = field.reshape(2, VARS, depth, slots, rows)

    def rates(state, offset):
        mats = jnp.stack(
            [
                matching(mode_source[0], mode_target[0], mode_count[0], offset, 1.0),
                matching(mode_source[1], mode_target[1], mode_count[1], offset, -1.0),
            ]
        )
        planes = jnp.stack([state[0, :, -1], state[1, :, 0]])
        outgoing = jnp.transpose(planes.reshape(2, VARS, slots, per_band, owned), (3, 0, 1, 2, 4))
        buffer = jnp.zeros((devices, 2, VARS, slots, owned), jnp.float32)
        buffer = lax.dynamic_update_slice_in_dim(buffer, outgoing, band * per_band, 0)
        arrived = lax.all_to_all(buffer, "sector", split_axis=0, concat_axis=0, tiled=True)
        arrived = jnp.roll(arrived, half_band, axis=0).reshape(sectors, NB, 2, VARS, slots, owned)
        picked = lax.dynamic_index_in_dim(arrived, cell_band, 1, keepdims=False)
        banded = jnp.transpose(picked, (1, 2, 4, 0, 3)).reshape(2, VARS, owned, sectors * slots)
        band_ghosts = transform(banded, left_char, right_char, mats, forward, inverse)
        reply = jnp.transpose(band_ghosts.reshape(2, VARS, owned, sectors, slots), (3, 0, 1, 4, 2))
        back = jnp.zeros((sectors, NB, 2, VARS, slots, owned), jnp.float32)
        back = lax.dynamic_update_index_in_dim(back, reply, cell_band, 1)
        back = jnp.roll(back.reshape(devices, 2, VARS, slots, owned), -half_band, axis=0)
        returned = lax.all_to_all(back, "sector", split_axis=0, concat_axis=0, tiled=True)
        mine = lax.dynamic_slice_in_dim(returned, band * per_band, per_band, 0)
        ghosts = jnp.transpose(mine, (1, 2, 3, 0, 4)).reshape(2, VARS, slots, rows)
        before = passed_along(state[:, :, :, -1:], "sector", NB)
        after = passed_along(state[:, :, :, :1], "sector", -NB)
        cycle = jnp.concatenate([before, state, after], axis=3)
        widened = with_halo(state, (("sector", 4),), 1)
        radial = jnp.concatenate(
            [widened[..., :1] * low_keep, widened[..., 1:-1], widened[..., -1:] * high_keep], axis=4
        )
        return stencil(state, cycle, radial, ghosts, axial_jac, circ_jac)

    first = rates(grid, section_offset[0])
    second = rates(grid + 0.5 * time_step * first, section_offset[1])
    third = rates(grid + 0.5 * time_step * second, section_offset[2])
    fourth = rates(grid + time_step * third, section_offset[3])
    result = grid + time_step / 6.0 * (first + 2.0 * second + 2.0 * third + fourth)
    return result.reshape(field.shape)


ROWS = 32
LANES = 128
RADIAL = 16
PER_ROW = LANES // RADIAL
HALF = ROWS * PER_ROW
STATE_STEP = (0.5 * time_step, 0.5 * time_step, time_step)
SUM_STEP = (time_step / 6.0, time_step / 3.0, time_step / 3.0, time_step / 6.0)


def split(x):
    high = x.astype(jnp.bfloat16)
    return high, (x - high.astype(jnp.float32)).astype(jnp.bfloat16)


def split_tables():
    point = np.arange(2 * HALF).reshape(2, ROWS, PER_ROW).transpose(0, 2, 1).reshape(2, HALF)
    modes = np.arange(K)
    phase = 2.0 * np.pi * ((point[:, :, None] * modes) % NTH) / NTH
    weights = np.where(modes == 0, 1.0 / NTH, 2.0 / NTH)
    forward = np.concatenate([np.cos(phase), -np.sin(phase)], axis=2).transpose(0, 2, 1)
    inverse = np.concatenate([weights * np.cos(phase), -weights * np.sin(phase)], axis=2)

    def both(x):
        high = x.astype(jnp.bfloat16)
        low = (x - high.astype(np.float64)).astype(jnp.bfloat16)
        return np.stack([high, low], axis=1)

    return both(forward), both(inverse)


def dot3(a_high, a_low, b):
    b_high, b_low = split(b)
    dot = functools.partial(jnp.dot, preferred_element_type=jnp.float32)
    return dot(a_high, b_high) + (dot(a_high, b_low) + dot(a_low, b_high))


def turned(x, shift, axis=1):
    if isinstance(shift, int):
        shift = shift % x.shape[axis]
        return x if shift == 0 else pltpu.roll(x, shift, axis)
    return pltpu.roll(x, lax.rem(shift + 2 * LANES, LANES), axis)


def packed(planes):
    group = lax.broadcasted_iota(jnp.int32, (ROWS, LANES), 1) // RADIAL
    parts = []
    for c in range(PER_ROW):
        part = jnp.zeros((ROWS, LANES), jnp.float32)
        for v in range(VARS):
            part = jnp.where(group == v, turned(planes[v], RADIAL * (v - c)), part)
        parts.append(part)
    return jnp.concatenate(parts, axis=0)


def unpacked(x, v):
    group = lax.broadcasted_iota(jnp.int32, (ROWS, LANES), 1) // RADIAL
    plane = turned(x[:ROWS], -RADIAL * v)
    for c in range(1, PER_ROW):
        piece = turned(x[c * ROWS:(c + 1) * ROWS], RADIAL * (c - v))
        plane = jnp.where(group == c, piece, plane)
    return plane


def step_kernel(
    field_hbm, axial_hbm, circ_hbm, left_hbm, right_hbm, count_hbm, offset_hbm,
    source_hbm, target_hbm, forward_hbm, inverse_hbm, out,
    field, axial_jac, circ_jac, left_char, right_char, count, offset,
    source, target, forward, inverse,
    state, seam_in, radial_out, radial_in, circ_out, circ_in,
    rim_out, rim_in, corner_out, corner_in,
    gather, phases, ghost_map, spectrum, factors,
    load_sem, seam_send, seam_recv, radial_send, radial_recv, circ_send, circ_recv,
    rim_send, rim_recv, corner_send, corner_recv,
):
    depth = field.shape[2]
    devices = 2 * NB
    me = lax.axis_index("sector")
    position = lax.rem(me + NB // 2, devices)
    sector = position // NB
    band = lax.rem(position, NB)
    right = lax.rem(me + 1, devices)
    left = lax.rem(me + devices - 1, devices)
    partner = lax.rem(me + NB, devices)
    has_left, has_right = band > 0, band < NB - 1

    pairs = [(field_hbm.at[r], state.at[0, r, :, pl.ds(1, depth)]) for r in range(2)]
    pairs += [
        (field_hbm, field), (axial_hbm, axial_jac), (circ_hbm, circ_jac), (left_hbm, left_char),
        (right_hbm, right_char), (count_hbm, count), (offset_hbm, offset), (source_hbm, source),
        (target_hbm, target), (forward_hbm, forward), (inverse_hbm, inverse),
    ]
    loads = [pltpu.make_async_copy(a, b, load_sem.at[i]) for i, (a, b) in enumerate(pairs)]
    for load in loads:
        load.start()

    barrier = pltpu.get_barrier_semaphore()
    for other in (left, right, partner):
        pl.semaphore_signal(
            barrier, inc=1, device_id={"sector": other}, device_id_type=pl.DeviceIdType.MESH
        )

    lane = lax.broadcasted_iota(jnp.int32, (ROWS, LANES), 1)
    row = lax.broadcasted_iota(jnp.int32, (ROWS, LANES), 0)
    radial = lane % RADIAL
    lane1 = lax.broadcasted_iota(jnp.int32, (1, LANES), 1)
    group1 = lane1 // RADIAL

    def edge_rows(new):
        last = jnp.zeros((1, LANES), jnp.float32)
        first = jnp.zeros((1, LANES), jnp.float32)
        for v in range(VARS):
            last = jnp.where(group1 == v, turned(new[v][ROWS - 1:], RADIAL * (v + 1)), last)
            first = jnp.where(group1 == v, turned(new[v][:1], RADIAL * v), first)
        return last, first

    def pack(slot, r, a, new):
        here = radial == a
        for v in range(VARS):
            radial_out[slot, r, 0, v] = jnp.where(
                here, turned(new[v], a - (RADIAL - 1)), radial_out[slot, r, 0, v]
            )
            radial_out[slot, r, 1, v] = jnp.where(
                here, turned(new[v], a), radial_out[slot, r, 1, v]
            )
        last, first = edge_rows(new)
        circ_out[slot, r, 0, pl.ds(a, 1), :] = last
        circ_out[slot, r, 1, pl.ds(a, 1), :] = first

    def pack_edges(slot, planes):
        outer = jnp.zeros((ROWS, LANES), jnp.float32)
        inner = jnp.zeros((ROWS, LANES), jnp.float32)
        rows = []
        for r in range(2):
            for v in range(VARS):
                place = r * VARS + v
                outer = jnp.where(
                    radial == place, turned(planes[r][v], place - (RADIAL - 1)), outer
                )
                inner = jnp.where(radial == place, turned(planes[r][v], place), inner)
            rows += edge_rows(planes[r])
        rim_out[slot, 0] = outer
        rim_out[slot, 1] = inner
        corner_out[slot] = jnp.concatenate(rows + [jnp.zeros((4, LANES), jnp.float32)], axis=0)

    def remote(src, dst, send, recv, device):
        return pltpu.make_async_remote_copy(
            src_ref=src, dst_ref=dst, send_sem=send, recv_sem=recv,
            device_id={"sector": device}, device_id_type=pl.DeviceIdType.MESH,
        )

    def seams(k, cur):
        return [
            remote(
                state.at[cur, d, :, depth if d == 0 else 1], seam_in.at[k, d],
                seam_send.at[k, d], seam_recv.at[k, d], partner,
            )
            for d in range(2)
        ]

    def sides(k, r):
        return [
            remote(
                radial_out.at[k, r, d], radial_in.at[k, r, d], radial_send.at[k, r, d],
                radial_recv.at[k, r, d], right if d == 0 else left,
            )
            for d in range(2)
        ]

    def rims(k):
        return [
            remote(
                rim_out.at[k, d], rim_in.at[k, d], rim_send.at[k, d], rim_recv.at[k, d],
                right if d == 0 else left,
            )
            for d in range(2)
        ]

    def circs(k, r):
        return remote(
            circ_out.at[k, r], circ_in.at[k, r], circ_send.at[k, r], circ_recv.at[k, r], partner
        )

    def corners(k):
        return remote(
            corner_out.at[k], corner_in.at[k], corner_send.at[k], corner_recv.at[k], partner
        )

    def send(sideways, across):
        for d, there in enumerate((has_right, has_left)):
            pl.when(there)(sideways[d].start)
        across.start()

    def arrive(sideways, across):
        for d, there in enumerate((has_left, has_right)):
            pl.when(there)(sideways[d].wait_recv)
        across.wait_recv()

    def sent(sideways, across):
        for d, there in enumerate((has_right, has_left)):
            pl.when(there)(sideways[d].wait_send)
        across.wait_send()

    def tables():
        wide = lax.broadcasted_iota(jnp.int32, (K, K), 0)
        pair = lax.broadcasted_iota(jnp.int32, (K, K), 1)
        for d in range(2):
            from_source = (source[d:d + 1, :] == wide).astype(jnp.float32).astype(jnp.bfloat16)
            to_target = jnp.where(
                (target[d:d + 1, :] == wide) & (pair < count[d]), 1.0, 0.0
            ).astype(jnp.bfloat16)
            moves = lax.dot_general(
                to_target, from_source, (((1,), (1,)), ((), ())),
                preferred_element_type=jnp.float32,
            ).astype(jnp.bfloat16)
            for part in range(2):
                for wave in range(2):
                    gather[d, part, :, wave * K:(wave + 1) * K] = jnp.dot(
                        inverse[sector, part, :, wave * K:(wave + 1) * K], moves,
                        preferred_element_type=jnp.float32,
                    ).astype(jnp.bfloat16)
            for v in range(VARS):
                for w in range(VARS):
                    total = right_char[v, d, 0] * left_char[0, d, w]
                    for c in range(1, VARS):
                        total = total + right_char[v, d, c] * left_char[c, d, w]
                    ghost_map[d, v * VARS + w] = total
                    factors[0, d, v * VARS + w] = -0.5 * axial_jac[v, d, w]
                    factors[1, d, v * VARS + w] = -0.5 * circ_jac[v, d, w]
        mode = lax.broadcasted_iota(jnp.int32, (K, LANES), 0)
        for s in range(4):
            angle = ((mode * offset[s]) & (NTH - 1)).astype(jnp.float32) * (2.0 * math.pi / NTH)
            phases[s, 0] = jnp.cos(angle)
            phases[s, 1] = jnp.sin(angle)

    def own_spectrum(cur):
        both = jnp.concatenate(
            [
                packed([state[cur, 0, v, depth] for v in range(VARS)]),
                packed([state[cur, 1, v, 1] for v in range(VARS)]),
            ],
            axis=1,
        )
        spectrum[...] = dot3(forward[sector, 0], forward[sector, 1], both)

    def make_ghosts(k, cur):
        both = jnp.concatenate(
            [packed([seam_in[k, d, v] for v in range(VARS)]) for d in range(2)], axis=1
        )
        whole = spectrum[...] + dot3(forward[1 - sector, 0], forward[1 - sector, 1], both)
        cosine, sine = phases[k, 0], phases[k, 1]
        for d in range(2):
            even = whole[:K, d * LANES:(d + 1) * LANES]
            odd = whole[K:, d * LANES:(d + 1) * LANES]
            turn = sine if d == 0 else -sine
            moved = jnp.concatenate([cosine * even - turn * odd, turn * even + cosine * odd], axis=0)
            raw = dot3(gather[d, 0], gather[d, 1], moved)
            planes = [unpacked(raw, w) for w in range(VARS)]
            for v in range(VARS):
                ghost = ghost_map[d, v * VARS] * planes[0]
                for w in range(1, VARS):
                    ghost = ghost + ghost_map[d, v * VARS + w] * planes[w]
                if d == 0:
                    state[cur, 1, v, 0] = ghost
                else:
                    state[cur, 0, v, depth + 1] = ghost

    def advance(k, cur, r, a, last, edge):
        if edge:
            up_row = corner_in[k, 2 * r:2 * r + 1, :]
            down_row = corner_in[k, 2 * r + 1:2 * r + 2, :]
        else:
            up_row = circ_in[k, r, 0, pl.ds(a, 1), :]
            down_row = circ_in[k, r, 1, pl.ds(a, 1), :]
        along, around, spread = [], [], []
        for w in range(VARS):
            x = state[cur, r, w, a + 1]
            before, after = state[cur, r, w, a], state[cur, r, w, a + 2]
            up = jnp.where(row == 0, turned(up_row, LANES - RADIAL - RADIAL * w), turned(x, 1, 0))
            down = jnp.where(row == ROWS - 1, turned(down_row, -RADIAL * w), turned(x, -1, 0))
            previous = turned(jnp.where(lane >= LANES - RADIAL, up, x), RADIAL)
            following = turned(jnp.where(lane < RADIAL, down, x), -RADIAL)
            if edge:
                place = r * VARS + w
                low, high = turned(rim_in[k, 0], -place), turned(rim_in[k, 1], RADIAL - 1 - place)
            else:
                low = turned(radial_in[k, r, 0, w], -a)
                high = turned(radial_in[k, r, 1, w], RADIAL - 1 - a)
            inner = jnp.where(radial == 0, low, turned(x, 1))
            outer = jnp.where(radial == RADIAL - 1, high, turned(x, -1))
            along.append(after - before)
            around.append(following - previous)
            spread.append(
                diffusion * ((after + before) + (following + previous) + (inner + outer) - 6.0 * x)
            )
        if last:
            sum_step = SUM_STEP[3]
        else:
            state_step = jnp.where(k == 2, STATE_STEP[2], STATE_STEP[0])
            sum_step = jnp.where(k == 0, SUM_STEP[0], SUM_STEP[1])
        new = []
        for v in range(VARS):
            rate = spread[v]
            for w in range(VARS):
                rate = rate + factors[0, r, v * VARS + w] * along[w]
                rate = rate + factors[1, r, v * VARS + w] * around[w]
            if last:
                out[r, v, a] = out[r, v, a] + sum_step * rate
            else:
                base = field[r, v, a]
                total = jnp.where(k == 0, base, out[r, v, a])
                out[r, v, a] = total + sum_step * rate
                n = base + state_step * rate
                state[1 - cur, r, v, a + 1] = n
                new.append(n)
        return new

    def stage(k, last=False):
        cur = k % 2 if isinstance(k, int) else lax.rem(k, 2)
        for r in range(2):
            arrive(sides(k, r), circs(k, r))

            def inside(a, carry):
                new = advance(k, cur, r, a, last, False)
                if not last:
                    pack(k + 1, r, a, new)
                return carry

            lax.fori_loop(r, depth - 1 + r, inside, 0)
            if not last:
                send(sides(k + 1, r), circs(k + 1, r))
        for copy in seams(k, cur):
            copy.wait_recv()
        make_ghosts(k, cur)
        arrive(rims(k), corners(k))
        planes = [advance(k, cur, r, (depth - 1) * (1 - r), last, True) for r in range(2)]
        if not last:
            for copy in seams(k + 1, 1 - cur):
                copy.start()
            pack_edges(k + 1, planes)
            send(rims(k + 1), corners(k + 1))
            own_spectrum(1 - cur)
        for copy in seams(k, cur):
            copy.wait_send()

    for d, there in enumerate((has_left, has_right)):

        @pl.when(jnp.logical_not(there))
        def _():
            for k in range(4):
                rim_in[k, d] = jnp.zeros((ROWS, LANES), jnp.float32)
                for r in range(2):
                    radial_in[k, r, d] = jnp.zeros((VARS, ROWS, LANES), jnp.float32)

    for slot in range(2):
        for v in range(VARS):
            state[slot, 0, v, 0] = jnp.zeros((ROWS, LANES), jnp.float32)
            state[slot, 1, v, depth + 1] = jnp.zeros((ROWS, LANES), jnp.float32)

    loads[0].wait()
    loads[1].wait()
    pl.semaphore_wait(barrier, 3)
    for r in range(2):

        def take_in(a, carry):
            pack(0, r, a, [state[0, r, v, a + 1] for v in range(VARS)])
            return carry

        lax.fori_loop(r, depth - 1 + r, take_in, 0)
        send(sides(0, r), circs(0, r))
        if r == 0:
            for copy in seams(0, 0):
                copy.start()
    pack_edges(
        0, [[state[0, 0, v, depth] for v in range(VARS)], [state[0, 1, v, 1] for v in range(VARS)]]
    )
    send(rims(0), corners(0))
    for load in loads[2:]:
        load.wait()
    tables()
    own_spectrum(0)

    def early(k, carry):
        stage(k)
        return carry

    lax.fori_loop(0, 3, early, 0)
    stage(3, last=True)
    for k in range(4):
        for r in range(2):
            sent(sides(k, r), circs(k, r))
        sent(rims(k), corners(k))


def fast_path(
    field, axial_jac, circ_jac, left_char, right_char, mode_source, mode_target, mode_count,
    section_offset,
):
    depth = field.shape[2]
    grid = field.reshape(2, VARS, depth, ROWS, LANES)
    forward, inverse = split_tables()
    plane = (ROWS, LANES)
    small = [jnp.transpose(m, (1, 0, 2)) for m in (axial_jac, circ_jac, left_char, right_char)]
    args = [
        grid, *small, mode_count, section_offset, mode_source, mode_target,
        jnp.asarray(forward), jnp.asarray(inverse),
    ]
    places = [pltpu.VMEM] + [pltpu.SMEM] * 6 + [pltpu.VMEM] * 4
    result = pl.pallas_call(
        step_kernel,
        out_shape=jax.ShapeDtypeStruct(grid.shape, jnp.float32),
        in_specs=[pl.BlockSpec(memory_space=pltpu.HBM)] * len(args),
        out_specs=pl.BlockSpec(memory_space=pltpu.VMEM),
        scratch_shapes=[place(x.shape, x.dtype) for place, x in zip(places, args)] + [
            pltpu.VMEM((2, 2, VARS, depth + 2) + plane, jnp.float32),
            pltpu.VMEM((4, 2, VARS) + plane, jnp.float32),
            pltpu.VMEM((4, 2, 2, VARS) + plane, jnp.float32),
            pltpu.VMEM((4, 2, 2, VARS) + plane, jnp.float32),
            pltpu.VMEM((4, 2, 2, depth, LANES), jnp.float32),
            pltpu.VMEM((4, 2, 2, depth, LANES), jnp.float32),
            pltpu.VMEM((4, 2) + plane, jnp.float32),
            pltpu.VMEM((4, 2) + plane, jnp.float32),
            pltpu.VMEM((4, 8, LANES), jnp.float32),
            pltpu.VMEM((4, 8, LANES), jnp.float32),
            pltpu.VMEM((2, 2, HALF, 2 * K), jnp.bfloat16),
            pltpu.VMEM((4, 2, K, LANES), jnp.float32),
            pltpu.SMEM((2, VARS * VARS), jnp.float32),
            pltpu.VMEM((2 * K, 2 * LANES), jnp.float32),
            pltpu.SMEM((2, 2, VARS * VARS), jnp.float32),
            pltpu.SemaphoreType.DMA((len(args) + 2,)),
            pltpu.SemaphoreType.DMA((4, 2)),
            pltpu.SemaphoreType.DMA((4, 2)),
            pltpu.SemaphoreType.DMA((4, 2, 2)),
            pltpu.SemaphoreType.DMA((4, 2, 2)),
            pltpu.SemaphoreType.DMA((4, 2)),
            pltpu.SemaphoreType.DMA((4, 2)),
            pltpu.SemaphoreType.DMA((4, 2)),
            pltpu.SemaphoreType.DMA((4, 2)),
            pltpu.SemaphoreType.DMA((4,)),
            pltpu.SemaphoreType.DMA((4,)),
        ],
        compiler_params=pltpu.CompilerParams(
            collective_id=0, has_side_effects=True, vmem_limit_bytes=62 * 1024 * 1024
        ),
    )(*args)
    return result.reshape(field.shape)


def on_device(field, *rest):
    fits = lax.axis_size("sector") == 2 * NB and field.shape[4] == ROWS * LANES
    return (fast_path if fits else general_path)(field, *rest)


def solution(mesh):
    in_specs = (P("group", None, None, "sector", None), P(), P(), P(), P(), P(), P(), P(), P())
    out_specs = P("group", None, None, "sector", None)
    return jax.shard_map(
        on_device, mesh=mesh, in_specs=in_specs, out_specs=out_specs, check_vma=False
    )
```

```python
import functools
import math

import jax
import jax.numpy as jnp
import numpy as np
from jax import lax
from jax.experimental import pallas as pl
from jax.experimental.pallas import tpu as pltpu
from jax.sharding import PartitionSpec as P

NTH = 512
VARS = 5
NB = 8
NR = 128
K = 256


precise = lax.Precision.HIGHEST
time_step = 0.2
diffusion = 0.05


def passed_along(block, axis, distance):
    devices = range(lax.axis_size(axis))
    route = [((i - distance) % len(devices), i) for i in devices]
    return lax.ppermute(block, axis, route)


def with_halo(x, sides, width):
    for axis, dim in sides:
        size, length = (lax.axis_size(axis), x.shape[dim])
        up = [(i, (i + 1) % size) for i in range(size)]
        down = [(j, i) for i, j in up]
        last = lax.slice_in_dim(x, length - width, length, axis=dim)
        first = lax.slice_in_dim(x, 0, width, axis=dim)
        before = lax.ppermute(last, axis, up)
        after = lax.ppermute(first, axis, down)
        x = jnp.concatenate([before, x, after], axis=dim)
    return x


def fourier_tables():
    theta = jnp.arange(NTH, dtype=jnp.int32)
    modes = jnp.arange(K, dtype=jnp.int32)
    phase = (theta[:, None] * modes[None, :] % NTH).astype(jnp.float32) * (2.0 * math.pi / NTH)
    cosine = jnp.cos(phase)
    sine = jnp.sin(phase)
    forward = jnp.concatenate([cosine, -sine], axis=1)
    weights = jnp.where(modes == 0, 1.0 / NTH, 2.0 / NTH).astype(jnp.float32)
    inverse = jnp.concatenate([(cosine * weights[None, :]).T, -(sine * weights[None, :]).T], axis=0)
    return (forward, inverse)


def matching(source, target, count, offset, sign):
    modes = jnp.arange(K, dtype=jnp.int32)
    valid = (modes < count).astype(jnp.float32)
    phase = (source * offset % NTH).astype(jnp.float32) * (sign * 2.0 * math.pi / NTH)
    weighted_cos = jnp.cos(phase) * valid
    weighted_sin = jnp.sin(phase) * valid
    one_source = (source[:, None] == modes[None, :]).astype(jnp.float32)
    one_target = (target[:, None] == modes[None, :]).astype(jnp.float32)
    keep = jnp.dot(one_source.T, weighted_cos[:, None] * one_target, precision=precise)
    turn = jnp.dot(one_source.T, weighted_sin[:, None] * one_target, precision=precise)
    return jnp.concatenate([jnp.concatenate([keep, turn], 1), jnp.concatenate([-turn, keep], 1)], 0)


def transform(planes, left_char, right_char, mats, forward, inverse):
    spectrum = jnp.einsum("dvrt,tk->dvrk", planes, forward, precision=precise)
    charac = jnp.einsum("dwv,dvrk->dwrk", left_char, spectrum, precision=precise)
    moved = jnp.einsum("dwrk,dkm->dwrm", charac, mats, precision=precise)
    back = jnp.einsum("dvw,dwrm->dvrm", right_char, moved, precision=precise)
    return jnp.einsum("dvrm,mt->dvrt", back, inverse, precision=precise)


def stencil(state, cycle, radial, ghosts, axial_jac, circ_jac):
    zero = jnp.zeros_like(ghosts[0])
    lower = jnp.stack([zero, ghosts[0]])
    upper = jnp.stack([ghosts[1], zero])
    axial = jnp.concatenate([lower[:, :, None], state, upper[:, :, None]], axis=2)
    d_axial = (axial[:, :, 2:] - axial[:, :, :-2]) * 0.5
    d_circ = (cycle[:, :, :, 2:] - cycle[:, :, :, :-2]) * 0.5
    neighbours = axial[:, :, 2:] + axial[:, :, :-2] + cycle[:, :, :, 2:] + cycle[:, :, :, :-2]
    neighbours = neighbours + radial[..., 2:] + radial[..., :-2]
    flux = jnp.einsum("rvw,rwatn->rvatn", axial_jac, d_axial, precision=precise)
    flux = flux + jnp.einsum("rvw,rwatn->rvatn", circ_jac, d_circ, precision=precise)
    return -flux + diffusion * (neighbours - 6.0 * state)


def general_path(
    field,
    axial_jac,
    circ_jac,
    left_char,
    right_char,
    mode_source,
    mode_target,
    mode_count,
    section_offset,
):
    forward, inverse = fourier_tables()
    devices = lax.axis_size("sector")
    index = lax.axis_index("sector")
    depth = field.shape[2]
    rows = NR // NB
    slots = field.shape[4] // rows
    sectors = devices // NB
    per_band = devices // NB
    owned = NR // devices
    half_band = NB // 2
    position = (index + half_band) % devices
    band = position % NB
    cell_band = index // per_band
    low_keep = (band > 0).astype(jnp.float32)
    high_keep = (band < NB - 1).astype(jnp.float32)
    grid = field.reshape(2, VARS, depth, slots, rows)

    def rates(state, offset):
        mats = jnp.stack(
            [
                matching(mode_source[0], mode_target[0], mode_count[0], offset, 1.0),
                matching(mode_source[1], mode_target[1], mode_count[1], offset, -1.0),
            ]
        )
        planes = jnp.stack([state[0, :, -1], state[1, :, 0]])
        outgoing = jnp.transpose(planes.reshape(2, VARS, slots, per_band, owned), (3, 0, 1, 2, 4))
        buffer = jnp.zeros((devices, 2, VARS, slots, owned), jnp.float32)
        buffer = lax.dynamic_update_slice_in_dim(buffer, outgoing, band * per_band, 0)
        arrived = lax.all_to_all(buffer, "sector", split_axis=0, concat_axis=0, tiled=True)
        arrived = jnp.roll(arrived, half_band, axis=0).reshape(sectors, NB, 2, VARS, slots, owned)
        picked = lax.dynamic_index_in_dim(arrived, cell_band, 1, keepdims=False)
        banded = jnp.transpose(picked, (1, 2, 4, 0, 3)).reshape(2, VARS, owned, sectors * slots)
        band_ghosts = transform(banded, left_char, right_char, mats, forward, inverse)
        reply = jnp.transpose(band_ghosts.reshape(2, VARS, owned, sectors, slots), (3, 0, 1, 4, 2))
        back = jnp.zeros((sectors, NB, 2, VARS, slots, owned), jnp.float32)
        back = lax.dynamic_update_index_in_dim(back, reply, cell_band, 1)
        back = jnp.roll(back.reshape(devices, 2, VARS, slots, owned), -half_band, axis=0)
        returned = lax.all_to_all(back, "sector", split_axis=0, concat_axis=0, tiled=True)
        mine = lax.dynamic_slice_in_dim(returned, band * per_band, per_band, 0)
        ghosts = jnp.transpose(mine, (1, 2, 3, 0, 4)).reshape(2, VARS, slots, rows)
        before = passed_along(state[:, :, :, -1:], "sector", NB)
        after = passed_along(state[:, :, :, :1], "sector", -NB)
        cycle = jnp.concatenate([before, state, after], axis=3)
        widened = with_halo(state, (("sector", 4),), 1)
        radial = jnp.concatenate(
            [widened[..., :1] * low_keep, widened[..., 1:-1], widened[..., -1:] * high_keep], axis=4
        )
        return stencil(state, cycle, radial, ghosts, axial_jac, circ_jac)

    first = rates(grid, section_offset[0])
    second = rates(grid + 0.5 * time_step * first, section_offset[1])
    third = rates(grid + 0.5 * time_step * second, section_offset[2])
    fourth = rates(grid + time_step * third, section_offset[3])
    result = grid + time_step / 6.0 * (first + 2.0 * second + 2.0 * third + fourth)
    return result.reshape(field.shape)


ROWS = 32
LANES = 128
RADIAL = 16
PER_ROW = LANES // RADIAL
HALF = ROWS * PER_ROW
STATE_STEP = (0.5 * time_step, 0.5 * time_step, time_step)
TILE = 8
TOGETHER = 4


def split(x):
    high = x.astype(jnp.bfloat16)
    return high, (x - high.astype(jnp.float32)).astype(jnp.bfloat16)


def split_tables():
    point = np.arange(2 * HALF).reshape(2, ROWS, PER_ROW).transpose(0, 2, 1).reshape(2, HALF)
    modes = np.arange(K)
    phase = 2.0 * np.pi * ((point[:, :, None] * modes) % NTH) / NTH
    weights = np.where(modes == 0, 1.0 / NTH, 2.0 / NTH)
    forward = np.concatenate([np.cos(phase), -np.sin(phase)], axis=2).transpose(0, 2, 1)
    inverse = np.concatenate([weights * np.cos(phase), -weights * np.sin(phase)], axis=2)

    def both(x):
        high = x.astype(jnp.bfloat16)
        low = (x - high.astype(np.float64)).astype(jnp.bfloat16)
        return np.stack([high, low], axis=1)

    return both(forward), both(inverse)


def dot3(a_high, a_low, b):
    b_high, b_low = split(b)
    dot = functools.partial(jnp.dot, preferred_element_type=jnp.float32)
    return dot(a_high, b_high) + (dot(a_high, b_low) + dot(a_low, b_high))


def turned(x, shift, axis=1):
    if isinstance(shift, int):
        shift = shift % x.shape[axis]
        return x if shift == 0 else pltpu.roll(x, shift, axis)
    return pltpu.roll(x, lax.rem(shift + 2 * LANES, LANES), axis)


def packed(planes):
    group = lax.broadcasted_iota(jnp.int32, (ROWS, LANES), 1) // RADIAL
    parts = []
    for c in range(PER_ROW):
        part = jnp.zeros((ROWS, LANES), jnp.float32)
        for v in range(VARS):
            part = jnp.where(group == v, turned(planes[v], RADIAL * (v - c)), part)
        parts.append(part)
    return jnp.concatenate(parts, axis=0)


def unpacked(x, v):
    group = lax.broadcasted_iota(jnp.int32, (ROWS, LANES), 1) // RADIAL
    plane = turned(x[:ROWS], -RADIAL * v)
    for c in range(1, PER_ROW):
        piece = turned(x[c * ROWS:(c + 1) * ROWS], RADIAL * (c - v))
        plane = jnp.where(group == c, piece, plane)
    return plane


def step_kernel(
    field_hbm, axial_hbm, circ_hbm, left_hbm, right_hbm, count_hbm, offset_hbm,
    source_hbm, target_hbm, forward_hbm, inverse_hbm, out,
    axial_jac, circ_jac, left_char, right_char, count, offset,
    source, target, forward, inverse,
    state, seam_in, radial_out, radial_in, circ_out, circ_in,
    rim_out, rim_in, corner_out, corner_in,
    gather, phases, ghost_map, spectrum, factors,
    load_sem, seam_send, seam_recv, radial_send, radial_recv, circ_send, circ_recv,
    rim_send, rim_recv, corner_send, corner_recv,
):
    depth = out.shape[2]
    devices = 2 * NB
    me = lax.axis_index("sector")
    position = lax.rem(me + NB // 2, devices)
    sector = position // NB
    band = lax.rem(position, NB)
    right = lax.rem(me + 1, devices)
    left = lax.rem(me + devices - 1, devices)
    partner = lax.rem(me + NB, devices)
    has_left, has_right = band > 0, band < NB - 1

    pairs = [(field_hbm.at[r], state.at[0, r, :, pl.ds(1, depth)]) for r in range(2)]
    pairs += [
        (axial_hbm, axial_jac), (circ_hbm, circ_jac), (left_hbm, left_char),
        (right_hbm, right_char), (count_hbm, count), (offset_hbm, offset), (source_hbm, source),
        (target_hbm, target), (forward_hbm, forward), (inverse_hbm, inverse),
    ]
    loads = [pltpu.make_async_copy(a, b, load_sem.at[i]) for i, (a, b) in enumerate(pairs)]
    for load in loads:
        load.start()

    barrier = pltpu.get_barrier_semaphore()
    for other in (left, right, partner):
        pl.semaphore_signal(
            barrier, inc=1, device_id={"sector": other}, device_id_type=pl.DeviceIdType.MESH
        )

    lane = lax.broadcasted_iota(jnp.int32, (ROWS, LANES), 1)
    row = lax.broadcasted_iota(jnp.int32, (ROWS, LANES), 0)
    radial = lane % RADIAL
    lane1 = lax.broadcasted_iota(jnp.int32, (1, LANES), 1)
    group1 = lane1 // RADIAL

    row8 = lax.broadcasted_iota(jnp.int32, (TILE, LANES), 0)
    lane8 = lax.broadcasted_iota(jnp.int32, (TILE, LANES), 1)
    radial8 = lane8 % RADIAL
    at_last, at_first = lane8 >= LANES - RADIAL, lane8 < RADIAL

    def edge_rows(top, bottom):
        last = jnp.zeros((1, LANES), jnp.float32)
        first = jnp.zeros((1, LANES), jnp.float32)
        for v in range(VARS):
            last = jnp.where(group1 == v, turned(bottom[v], RADIAL * (v + 1)), last)
            first = jnp.where(group1 == v, turned(top[v], RADIAL * v), first)
        return last, first

    def pack_rows(slot, r, a, top, bottom):
        last, first = edge_rows(top, bottom)
        circ_out[slot, r, 0, pl.ds(a, 1), :] = last
        circ_out[slot, r, 1, pl.ds(a, 1), :] = first

    def pack(slot, r, a, new):
        here = radial == a
        for v in range(VARS):
            radial_out[slot, r, 0, v] = jnp.where(
                here, turned(new[v], a - (RADIAL - 1)), radial_out[slot, r, 0, v]
            )
            radial_out[slot, r, 1, v] = jnp.where(
                here, turned(new[v], a), radial_out[slot, r, 1, v]
            )
        pack_rows(slot, r, a, [n[:1] for n in new], [n[ROWS - 1:] for n in new])

    def pack_edges(slot):
        outer = jnp.zeros((ROWS, LANES), jnp.float32)
        inner = jnp.zeros((ROWS, LANES), jnp.float32)
        rows = []
        for r in range(2):
            planes = [state[slot, r, v, depth if r == 0 else 1] for v in range(VARS)]
            for v in range(VARS):
                place = r * VARS + v
                outer = jnp.where(radial == place, turned(planes[v], place - (RADIAL - 1)), outer)
                inner = jnp.where(radial == place, turned(planes[v], place), inner)
            rows += edge_rows([n[:1] for n in planes], [n[ROWS - 1:] for n in planes])
        rim_out[slot, 0] = outer
        rim_out[slot, 1] = inner
        corner_out[slot] = jnp.concatenate(rows + [jnp.zeros((4, LANES), jnp.float32)], axis=0)

    def remote(src, dst, send, recv, device):
        return pltpu.make_async_remote_copy(
            src_ref=src, dst_ref=dst, send_sem=send, recv_sem=recv,
            device_id={"sector": device}, device_id_type=pl.DeviceIdType.MESH,
        )

    def seams(k):
        return [
            remote(
                state.at[k, d, :, depth if d == 0 else 1], seam_in.at[k, d],
                seam_send.at[k, d], seam_recv.at[k, d], partner,
            )
            for d in range(2)
        ]

    def sides(k, r):
        return [
            remote(
                radial_out.at[k, r, d], radial_in.at[k, r, d], radial_send.at[k, r, d],
                radial_recv.at[k, r, d], right if d == 0 else left,
            )
            for d in range(2)
        ]

    def rims(k):
        return [
            remote(
                rim_out.at[k, d], rim_in.at[k, d], rim_send.at[k, d], rim_recv.at[k, d],
                right if d == 0 else left,
            )
            for d in range(2)
        ]

    def circs(k, r):
        return remote(
            circ_out.at[k, r], circ_in.at[k, r], circ_send.at[k, r], circ_recv.at[k, r], partner
        )

    def corners(k):
        return remote(
            corner_out.at[k], corner_in.at[k], corner_send.at[k], corner_recv.at[k], partner
        )

    def send(sideways, across):
        for d, there in enumerate((has_right, has_left)):
            pl.when(there)(sideways[d].start)
        across.start()

    def arrive(sideways, across):
        for d, there in enumerate((has_left, has_right)):
            pl.when(there)(sideways[d].wait_recv)
        across.wait_recv()

    def sent(sideways, across):
        for d, there in enumerate((has_right, has_left)):
            pl.when(there)(sideways[d].wait_send)
        across.wait_send()

    def tables():
        wide = lax.broadcasted_iota(jnp.int32, (K, K), 0)
        pair = lax.broadcasted_iota(jnp.int32, (K, K), 1)
        for d in range(2):
            from_source = (source[d:d + 1, :] == wide).astype(jnp.float32).astype(jnp.bfloat16)
            to_target = jnp.where(
                (target[d:d + 1, :] == wide) & (pair < count[d]), 1.0, 0.0
            ).astype(jnp.bfloat16)
            moves = lax.dot_general(
                to_target, from_source, (((1,), (1,)), ((), ())),
                preferred_element_type=jnp.float32,
            ).astype(jnp.bfloat16)
            for part in range(2):
                for wave in range(2):
                    gather[d, part, :, wave * K:(wave + 1) * K] = jnp.dot(
                        inverse[sector, part, :, wave * K:(wave + 1) * K], moves,
                        preferred_element_type=jnp.float32,
                    ).astype(jnp.bfloat16)
            for v in range(VARS):
                for w in range(VARS):
                    total = right_char[v, d, 0] * left_char[0, d, w]
                    for c in range(1, VARS):
                        total = total + right_char[v, d, c] * left_char[c, d, w]
                    ghost_map[d, v * VARS + w] = total
                    for which, jac in enumerate((axial_jac, circ_jac)):
                        factors[which, d, v * VARS + w] = jnp.full(
                            (TILE, LANES), (-0.5 / diffusion) * jac[v, d, w], jnp.float32
                        )
        mode = lax.broadcasted_iota(jnp.int32, (K, LANES), 0)
        for s in range(4):
            angle = ((mode * offset[s]) & (NTH - 1)).astype(jnp.float32) * (2.0 * math.pi / NTH)
            phases[s, 0] = jnp.cos(angle)
            phases[s, 1] = jnp.sin(angle)

    def own_spectrum(k):
        both = jnp.concatenate(
            [
                packed([state[k, 0, v, depth] for v in range(VARS)]),
                packed([state[k, 1, v, 1] for v in range(VARS)]),
            ],
            axis=1,
        )
        spectrum[...] = dot3(forward[sector, 0], forward[sector, 1], both)

    def make_ghosts(k):
        both = jnp.concatenate(
            [packed([seam_in[k, d, v] for v in range(VARS)]) for d in range(2)], axis=1
        )
        whole = spectrum[...] + dot3(forward[1 - sector, 0], forward[1 - sector, 1], both)
        cosine, sine = phases[k, 0], phases[k, 1]
        for d in range(2):
            even = whole[:K, d * LANES:(d + 1) * LANES]
            odd = whole[K:, d * LANES:(d + 1) * LANES]
            turn = sine if d == 0 else -sine
            moved = jnp.concatenate([cosine * even - turn * odd, turn * even + cosine * odd], axis=0)
            raw = dot3(gather[d, 0], gather[d, 1], moved)
            planes = [unpacked(raw, w) for w in range(VARS)]
            for v in range(VARS):
                ghost = ghost_map[d, v * VARS] * planes[0]
                for w in range(1, VARS):
                    ghost = ghost + ghost_map[d, v * VARS + w] * planes[w]
                if d == 0:
                    state[k, 1, v, 0] = ghost
                else:
                    state[k, 0, v, depth + 1] = ghost

    def advance(k, r, a, last, edge):
        tiles = range(ROWS // TILE)
        if edge:
            up_row = corner_in[k, 2 * r:2 * r + 1, :]
            down_row = corner_in[k, 2 * r + 1:2 * r + 2, :]
        else:
            up_row = circ_in[k, r, 0, pl.ds(a, 1), :]
            down_row = circ_in[k, r, 1, pl.ds(a, 1), :]
        if not last:
            step = jnp.where(k == 2, diffusion * STATE_STEP[2], diffusion * STATE_STEP[0])
        new = [[None] * len(tiles) for _ in range(VARS)]
        for start in range(0, len(tiles), TOGETHER):
            chunk = range(start, start + TOGETHER)
            along, around, rate = {}, {}, {}
            for w in range(VARS):
                for t in chunk:
                    lo = t * TILE
                    here = pl.ds(lo, TILE)
                    x = state[k, r, w, a + 1, here]
                    before, after = state[k, r, w, a, here], state[k, r, w, a + 2, here]
                    if t == 0:
                        halo = turned(up_row, LANES - RADIAL - RADIAL * w)
                        up = jnp.where(row8 == 0, halo, turned(x, 1, 0))
                    else:
                        up = state[k, r, w, a + 1, pl.ds(lo - 1, TILE)]
                    if t == tiles[-1]:
                        halo = turned(down_row, -RADIAL * w)
                        down = jnp.where(row8 == TILE - 1, halo, turned(x, -1, 0))
                    else:
                        down = state[k, r, w, a + 1, pl.ds(lo + 1, TILE)]
                    previous = turned(jnp.where(at_last, up, x), RADIAL)
                    following = turned(jnp.where(at_first, down, x), -RADIAL)
                    if edge:
                        place = r * VARS + w
                        low = turned(rim_in[k, 0, here], -place)
                        high = turned(rim_in[k, 1, here], RADIAL - 1 - place)
                    else:
                        low = turned(radial_in[k, r, 0, w, here], -a)
                        high = turned(radial_in[k, r, 1, w, here], RADIAL - 1 - a)
                    inner = jnp.where(radial8 == 0, low, turned(x, 1))
                    outer = jnp.where(radial8 == RADIAL - 1, high, turned(x, -1))
                    along[w, t] = after - before
                    around[w, t] = following - previous
                    rate[w, t] = (
                        (after + before) + (following + previous) + (inner + outer) - 6.0 * x
                    )
            for v in range(VARS):
                for w in range(VARS):
                    one, two = factors[0, r, v * VARS + w], factors[1, r, v * VARS + w]
                    for t in chunk:
                        rate[v, t] = rate[v, t] + (one * along[w, t] + two * around[w, t])
                for t in chunk:
                    here = pl.ds(t * TILE, TILE)
                    base = state[0, r, v, a + 1, here]
                    if last:
                        total = state[1, r, v, a + 1, here] + 2.0 * state[2, r, v, a + 1, here]
                        total = total + state[3, r, v, a + 1, here] - base
                        out[r, v, a, here] = (
                            total * (1.0 / 3.0) + (diffusion * time_step / 6.0) * rate[v, t]
                        )
                    else:
                        n = base + step * rate[v, t]
                        state[k + 1, r, v, a + 1, here] = n
                        new[v][t] = n
                        if not edge:
                            mine = radial8 == a
                            radial_out[k + 1, r, 0, v, here] = jnp.where(
                                mine, turned(n, a - (RADIAL - 1)), radial_out[k + 1, r, 0, v, here]
                            )
                            radial_out[k + 1, r, 1, v, here] = jnp.where(
                                mine, turned(n, a), radial_out[k + 1, r, 1, v, here]
                            )
        if not last and not edge:
            pack_rows(k + 1, r, a, [n[0][:1] for n in new], [n[-1][TILE - 1:] for n in new])
        return new

    def stage(k, last=False):
        for r in range(2):
            arrive(sides(k, r), circs(k, r))

            def inside(a, carry):
                advance(k, r, a, last, False)
                return carry

            lax.fori_loop(r, depth - 1 + r, inside, 0)
            if not last:
                send(sides(k + 1, r), circs(k + 1, r))
        for copy in seams(k):
            copy.wait_recv()
        make_ghosts(k)
        arrive(rims(k), corners(k))
        for r in range(2):
            advance(k, r, (depth - 1) * (1 - r), last, True)
        if not last:
            for copy in seams(k + 1):
                copy.start()
            pack_edges(k + 1)
            send(rims(k + 1), corners(k + 1))
            own_spectrum(k + 1)

    for d, there in enumerate((has_left, has_right)):

        @pl.when(jnp.logical_not(there))
        def _():
            for k in range(4):
                rim_in[k, d] = jnp.zeros((ROWS, LANES), jnp.float32)
                for r in range(2):
                    radial_in[k, r, d] = jnp.zeros((VARS, ROWS, LANES), jnp.float32)

    for slot in range(4):
        for v in range(VARS):
            state[slot, 0, v, 0] = jnp.zeros((ROWS, LANES), jnp.float32)
            state[slot, 1, v, depth + 1] = jnp.zeros((ROWS, LANES), jnp.float32)

    loads[0].wait()
    loads[1].wait()
    pl.semaphore_wait(barrier, 3)
    for copy in seams(0):
        copy.start()
    for r in range(2):

        def take_in(a, carry):
            pack(0, r, a, [state[0, r, v, a + 1] for v in range(VARS)])
            return carry

        lax.fori_loop(r, depth - 1 + r, take_in, 0)
        send(sides(0, r), circs(0, r))
    pack_edges(0)
    send(rims(0), corners(0))
    for load in loads[2:]:
        load.wait()
    tables()
    own_spectrum(0)

    def early(k, carry):
        stage(k)
        return carry

    lax.fori_loop(0, 3, early, 0)
    stage(3, last=True)
    for k in range(4):
        for copy in seams(k):
            copy.wait_send()
        for r in range(2):
            sent(sides(k, r), circs(k, r))
        sent(rims(k), corners(k))


def fast_path(
    field, axial_jac, circ_jac, left_char, right_char, mode_source, mode_target, mode_count,
    section_offset,
):
    depth = field.shape[2]
    grid = field.reshape(2, VARS, depth, ROWS, LANES)
    forward, inverse = split_tables()
    plane = (ROWS, LANES)
    small = [jnp.transpose(m, (1, 0, 2)) for m in (axial_jac, circ_jac, left_char, right_char)]
    args = [
        grid, *small, mode_count, section_offset, mode_source, mode_target,
        jnp.asarray(forward), jnp.asarray(inverse),
    ]
    places = [pltpu.SMEM] * 6 + [pltpu.VMEM] * 4
    result = pl.pallas_call(
        step_kernel,
        out_shape=jax.ShapeDtypeStruct(grid.shape, jnp.float32),
        in_specs=[pl.BlockSpec(memory_space=pltpu.HBM)] * len(args),
        out_specs=pl.BlockSpec(memory_space=pltpu.VMEM),
        scratch_shapes=[place(x.shape, x.dtype) for place, x in zip(places, args[1:])] + [
            pltpu.VMEM((4, 2, VARS, depth + 2) + plane, jnp.float32),
            pltpu.VMEM((4, 2, VARS) + plane, jnp.float32),
            pltpu.VMEM((4, 2, 2, VARS) + plane, jnp.float32),
            pltpu.VMEM((4, 2, 2, VARS) + plane, jnp.float32),
            pltpu.VMEM((4, 2, 2, depth, LANES), jnp.float32),
            pltpu.VMEM((4, 2, 2, depth, LANES), jnp.float32),
            pltpu.VMEM((4, 2) + plane, jnp.float32),
            pltpu.VMEM((4, 2) + plane, jnp.float32),
            pltpu.VMEM((4, 8, LANES), jnp.float32),
            pltpu.VMEM((4, 8, LANES), jnp.float32),
            pltpu.VMEM((2, 2, HALF, 2 * K), jnp.bfloat16),
            pltpu.VMEM((4, 2, K, LANES), jnp.float32),
            pltpu.SMEM((2, VARS * VARS), jnp.float32),
            pltpu.VMEM((2 * K, 2 * LANES), jnp.float32),
            pltpu.VMEM((2, 2, VARS * VARS, TILE, LANES), jnp.float32),
            pltpu.SemaphoreType.DMA((len(args) + 1,)),
            pltpu.SemaphoreType.DMA((4, 2)),
            pltpu.SemaphoreType.DMA((4, 2)),
            pltpu.SemaphoreType.DMA((4, 2, 2)),
            pltpu.SemaphoreType.DMA((4, 2, 2)),
            pltpu.SemaphoreType.DMA((4, 2)),
            pltpu.SemaphoreType.DMA((4, 2)),
            pltpu.SemaphoreType.DMA((4, 2)),
            pltpu.SemaphoreType.DMA((4, 2)),
            pltpu.SemaphoreType.DMA((4,)),
            pltpu.SemaphoreType.DMA((4,)),
        ],
        compiler_params=pltpu.CompilerParams(
            collective_id=0, has_side_effects=True, vmem_limit_bytes=62 * 1024 * 1024
        ),
    )(*args)
    return result.reshape(field.shape)


def on_device(field, *rest):
    fits = lax.axis_size("sector") == 2 * NB and field.shape[4] == ROWS * LANES
    return (fast_path if fits else general_path)(field, *rest)


def solution(mesh):
    in_specs = (P("group", None, None, "sector", None), P(), P(), P(), P(), P(), P(), P(), P())
    out_specs = P("group", None, None, "sector", None)
    return jax.shard_map(
        on_device, mesh=mesh, in_specs=in_specs, out_specs=out_specs, check_vma=False
    )
```

```python
import functools
import math

import jax
import jax.numpy as jnp
import numpy as np
from jax import lax
from jax.experimental import pallas as pl
from jax.experimental.pallas import tpu as pltpu
from jax.sharding import PartitionSpec as P

NTH = 512
VARS = 5
NB = 8
NR = 128
K = 256


precise = lax.Precision.HIGHEST
time_step = 0.2
diffusion = 0.05


def passed_along(block, axis, distance):
    devices = range(lax.axis_size(axis))
    route = [((i - distance) % len(devices), i) for i in devices]
    return lax.ppermute(block, axis, route)


def with_halo(x, sides, width):
    for axis, dim in sides:
        size, length = (lax.axis_size(axis), x.shape[dim])
        up = [(i, (i + 1) % size) for i in range(size)]
        down = [(j, i) for i, j in up]
        last = lax.slice_in_dim(x, length - width, length, axis=dim)
        first = lax.slice_in_dim(x, 0, width, axis=dim)
        before = lax.ppermute(last, axis, up)
        after = lax.ppermute(first, axis, down)
        x = jnp.concatenate([before, x, after], axis=dim)
    return x


def fourier_tables():
    theta = jnp.arange(NTH, dtype=jnp.int32)
    modes = jnp.arange(K, dtype=jnp.int32)
    phase = (theta[:, None] * modes[None, :] % NTH).astype(jnp.float32) * (2.0 * math.pi / NTH)
    cosine = jnp.cos(phase)
    sine = jnp.sin(phase)
    forward = jnp.concatenate([cosine, -sine], axis=1)
    weights = jnp.where(modes == 0, 1.0 / NTH, 2.0 / NTH).astype(jnp.float32)
    inverse = jnp.concatenate([(cosine * weights[None, :]).T, -(sine * weights[None, :]).T], axis=0)
    return (forward, inverse)


def matching(source, target, count, offset, sign):
    modes = jnp.arange(K, dtype=jnp.int32)
    valid = (modes < count).astype(jnp.float32)
    phase = (source * offset % NTH).astype(jnp.float32) * (sign * 2.0 * math.pi / NTH)
    weighted_cos = jnp.cos(phase) * valid
    weighted_sin = jnp.sin(phase) * valid
    one_source = (source[:, None] == modes[None, :]).astype(jnp.float32)
    one_target = (target[:, None] == modes[None, :]).astype(jnp.float32)
    keep = jnp.dot(one_source.T, weighted_cos[:, None] * one_target, precision=precise)
    turn = jnp.dot(one_source.T, weighted_sin[:, None] * one_target, precision=precise)
    return jnp.concatenate([jnp.concatenate([keep, turn], 1), jnp.concatenate([-turn, keep], 1)], 0)


def transform(planes, left_char, right_char, mats, forward, inverse):
    spectrum = jnp.einsum("dvrt,tk->dvrk", planes, forward, precision=precise)
    charac = jnp.einsum("dwv,dvrk->dwrk", left_char, spectrum, precision=precise)
    moved = jnp.einsum("dwrk,dkm->dwrm", charac, mats, precision=precise)
    back = jnp.einsum("dvw,dwrm->dvrm", right_char, moved, precision=precise)
    return jnp.einsum("dvrm,mt->dvrt", back, inverse, precision=precise)


def stencil(state, cycle, radial, ghosts, axial_jac, circ_jac):
    zero = jnp.zeros_like(ghosts[0])
    lower = jnp.stack([zero, ghosts[0]])
    upper = jnp.stack([ghosts[1], zero])
    axial = jnp.concatenate([lower[:, :, None], state, upper[:, :, None]], axis=2)
    d_axial = (axial[:, :, 2:] - axial[:, :, :-2]) * 0.5
    d_circ = (cycle[:, :, :, 2:] - cycle[:, :, :, :-2]) * 0.5
    neighbours = axial[:, :, 2:] + axial[:, :, :-2] + cycle[:, :, :, 2:] + cycle[:, :, :, :-2]
    neighbours = neighbours + radial[..., 2:] + radial[..., :-2]
    flux = jnp.einsum("rvw,rwatn->rvatn", axial_jac, d_axial, precision=precise)
    flux = flux + jnp.einsum("rvw,rwatn->rvatn", circ_jac, d_circ, precision=precise)
    return -flux + diffusion * (neighbours - 6.0 * state)


def general_path(
    field,
    axial_jac,
    circ_jac,
    left_char,
    right_char,
    mode_source,
    mode_target,
    mode_count,
    section_offset,
):
    forward, inverse = fourier_tables()
    devices = lax.axis_size("sector")
    index = lax.axis_index("sector")
    depth = field.shape[2]
    rows = NR // NB
    slots = field.shape[4] // rows
    sectors = devices // NB
    per_band = devices // NB
    owned = NR // devices
    half_band = NB // 2
    position = (index + half_band) % devices
    band = position % NB
    cell_band = index // per_band
    low_keep = (band > 0).astype(jnp.float32)
    high_keep = (band < NB - 1).astype(jnp.float32)
    grid = field.reshape(2, VARS, depth, slots, rows)

    def rates(state, offset):
        mats = jnp.stack(
            [
                matching(mode_source[0], mode_target[0], mode_count[0], offset, 1.0),
                matching(mode_source[1], mode_target[1], mode_count[1], offset, -1.0),
            ]
        )
        planes = jnp.stack([state[0, :, -1], state[1, :, 0]])
        outgoing = jnp.transpose(planes.reshape(2, VARS, slots, per_band, owned), (3, 0, 1, 2, 4))
        buffer = jnp.zeros((devices, 2, VARS, slots, owned), jnp.float32)
        buffer = lax.dynamic_update_slice_in_dim(buffer, outgoing, band * per_band, 0)
        arrived = lax.all_to_all(buffer, "sector", split_axis=0, concat_axis=0, tiled=True)
        arrived = jnp.roll(arrived, half_band, axis=0).reshape(sectors, NB, 2, VARS, slots, owned)
        picked = lax.dynamic_index_in_dim(arrived, cell_band, 1, keepdims=False)
        banded = jnp.transpose(picked, (1, 2, 4, 0, 3)).reshape(2, VARS, owned, sectors * slots)
        band_ghosts = transform(banded, left_char, right_char, mats, forward, inverse)
        reply = jnp.transpose(band_ghosts.reshape(2, VARS, owned, sectors, slots), (3, 0, 1, 4, 2))
        back = jnp.zeros((sectors, NB, 2, VARS, slots, owned), jnp.float32)
        back = lax.dynamic_update_index_in_dim(back, reply, cell_band, 1)
        back = jnp.roll(back.reshape(devices, 2, VARS, slots, owned), -half_band, axis=0)
        returned = lax.all_to_all(back, "sector", split_axis=0, concat_axis=0, tiled=True)
        mine = lax.dynamic_slice_in_dim(returned, band * per_band, per_band, 0)
        ghosts = jnp.transpose(mine, (1, 2, 3, 0, 4)).reshape(2, VARS, slots, rows)
        before = passed_along(state[:, :, :, -1:], "sector", NB)
        after = passed_along(state[:, :, :, :1], "sector", -NB)
        cycle = jnp.concatenate([before, state, after], axis=3)
        widened = with_halo(state, (("sector", 4),), 1)
        radial = jnp.concatenate(
            [widened[..., :1] * low_keep, widened[..., 1:-1], widened[..., -1:] * high_keep], axis=4
        )
        return stencil(state, cycle, radial, ghosts, axial_jac, circ_jac)

    first = rates(grid, section_offset[0])
    second = rates(grid + 0.5 * time_step * first, section_offset[1])
    third = rates(grid + 0.5 * time_step * second, section_offset[2])
    fourth = rates(grid + time_step * third, section_offset[3])
    result = grid + time_step / 6.0 * (first + 2.0 * second + 2.0 * third + fourth)
    return result.reshape(field.shape)


ROWS = 32
LANES = 128
RADIAL = 16
PER_ROW = LANES // RADIAL
HALF = ROWS * PER_ROW
STATE_STEP = (0.5 * time_step, 0.5 * time_step, time_step)
TILE = 8
TOGETHER = 4


def split(x):
    high = x.astype(jnp.bfloat16)
    return high, (x - high.astype(jnp.float32)).astype(jnp.bfloat16)


def split_tables():
    point = np.arange(2 * HALF).reshape(2, ROWS, PER_ROW).transpose(0, 2, 1).reshape(2, HALF)
    modes = np.arange(K)
    phase = 2.0 * np.pi * ((point[:, :, None] * modes) % NTH) / NTH
    weights = np.where(modes == 0, 1.0 / NTH, 2.0 / NTH)
    forward = np.concatenate([np.cos(phase), -np.sin(phase)], axis=2).transpose(0, 2, 1)
    inverse = np.concatenate([weights * np.cos(phase), -weights * np.sin(phase)], axis=2)

    def both(x):
        high = x.astype(jnp.bfloat16)
        low = (x - high.astype(np.float64)).astype(jnp.bfloat16)
        return np.stack([high, low], axis=1)

    return both(forward), both(inverse)


def dot3(a_high, a_low, b):
    b_high, b_low = split(b)
    dot = functools.partial(jnp.dot, preferred_element_type=jnp.float32)
    return dot(a_high, b_high) + (dot(a_high, b_low) + dot(a_low, b_high))


def turned(x, shift, axis=1):
    if isinstance(shift, int):
        shift = shift % x.shape[axis]
        return x if shift == 0 else pltpu.roll(x, shift, axis)
    return pltpu.roll(x, lax.rem(shift + 2 * LANES, LANES), axis)


def packed(planes):
    group = lax.broadcasted_iota(jnp.int32, (ROWS, LANES), 1) // RADIAL
    parts = []
    for c in range(PER_ROW):
        part = jnp.zeros((ROWS, LANES), jnp.float32)
        for v in range(VARS):
            part = jnp.where(group == v, turned(planes[v], RADIAL * (v - c)), part)
        parts.append(part)
    return jnp.concatenate(parts, axis=0)


def unpacked(x, v):
    group = lax.broadcasted_iota(jnp.int32, (ROWS, LANES), 1) // RADIAL
    plane = turned(x[:ROWS], -RADIAL * v)
    for c in range(1, PER_ROW):
        piece = turned(x[c * ROWS:(c + 1) * ROWS], RADIAL * (c - v))
        plane = jnp.where(group == c, piece, plane)
    return plane


def step_kernel(
    field_hbm, axial_hbm, circ_hbm, left_hbm, right_hbm, count_hbm, offset_hbm,
    source_hbm, target_hbm, forward_hbm, inverse_hbm, out,
    axial_jac, circ_jac, left_char, right_char, count, offset,
    source, target, forward, inverse,
    state, seam_in, radial_out, radial_in, circ_out, circ_in,
    rim_out, rim_in, corner_out, corner_in,
    gather, phases, ghost_map, spectrum, factors,
    load_sem, seam_send, seam_recv, radial_send, radial_recv, circ_send, circ_recv,
    rim_send, rim_recv, corner_send, corner_recv,
):
    depth = out.shape[2]
    devices = 2 * NB
    me = lax.axis_index("sector")
    position = lax.rem(me + NB // 2, devices)
    sector = position // NB
    band = lax.rem(position, NB)
    right = lax.rem(me + 1, devices)
    left = lax.rem(me + devices - 1, devices)
    partner = lax.rem(me + NB, devices)
    has_left, has_right = band > 0, band < NB - 1

    pairs = [(field_hbm.at[r], state.at[0, r, :, pl.ds(1, depth)]) for r in range(2)]
    pairs += [
        (axial_hbm, axial_jac), (circ_hbm, circ_jac), (left_hbm, left_char),
        (right_hbm, right_char), (count_hbm, count), (offset_hbm, offset), (source_hbm, source),
        (target_hbm, target), (forward_hbm, forward), (inverse_hbm, inverse),
    ]
    loads = [pltpu.make_async_copy(a, b, load_sem.at[i]) for i, (a, b) in enumerate(pairs)]
    for load in loads:
        load.start()

    barrier = pltpu.get_barrier_semaphore()
    for other in (left, right, partner):
        pl.semaphore_signal(
            barrier, inc=1, device_id={"sector": other}, device_id_type=pl.DeviceIdType.MESH
        )

    lane = lax.broadcasted_iota(jnp.int32, (ROWS, LANES), 1)
    row = lax.broadcasted_iota(jnp.int32, (ROWS, LANES), 0)
    radial = lane % RADIAL
    lane1 = lax.broadcasted_iota(jnp.int32, (1, LANES), 1)
    group1 = lane1 // RADIAL

    row8 = lax.broadcasted_iota(jnp.int32, (TILE, LANES), 0)
    lane8 = lax.broadcasted_iota(jnp.int32, (TILE, LANES), 1)
    radial8 = lane8 % RADIAL
    at_last, at_first = lane8 >= LANES - RADIAL, lane8 < RADIAL

    def edge_rows(top, bottom):
        last = jnp.zeros((1, LANES), jnp.float32)
        first = jnp.zeros((1, LANES), jnp.float32)
        for v in range(VARS):
            last = jnp.where(group1 == v, turned(bottom[v], RADIAL * (v + 1)), last)
            first = jnp.where(group1 == v, turned(top[v], RADIAL * v), first)
        return last, first

    def pack_rows(slot, r, a, top, bottom):
        last, first = edge_rows(top, bottom)
        circ_out[slot, r, 0, pl.ds(a, 1), :] = last
        circ_out[slot, r, 1, pl.ds(a, 1), :] = first

    def pack(slot, r, a, new):
        here = radial == a
        for v in range(VARS):
            radial_out[slot, r, 0, v] = jnp.where(
                here, turned(new[v], a - (RADIAL - 1)), radial_out[slot, r, 0, v]
            )
            radial_out[slot, r, 1, v] = jnp.where(
                here, turned(new[v], a), radial_out[slot, r, 1, v]
            )
        pack_rows(slot, r, a, [n[:1] for n in new], [n[ROWS - 1:] for n in new])

    def pack_edges(slot):
        outer = jnp.zeros((ROWS, LANES), jnp.float32)
        inner = jnp.zeros((ROWS, LANES), jnp.float32)
        rows = []
        for r in range(2):
            planes = [state[slot, r, v, depth if r == 0 else 1] for v in range(VARS)]
            for v in range(VARS):
                place = r * VARS + v
                outer = jnp.where(radial == place, turned(planes[v], place - (RADIAL - 1)), outer)
                inner = jnp.where(radial == place, turned(planes[v], place), inner)
            rows += edge_rows([n[:1] for n in planes], [n[ROWS - 1:] for n in planes])
        rim_out[slot, 0] = outer
        rim_out[slot, 1] = inner
        corner_out[slot] = jnp.concatenate(rows + [jnp.zeros((4, LANES), jnp.float32)], axis=0)

    def remote(src, dst, send, recv, device):
        return pltpu.make_async_remote_copy(
            src_ref=src, dst_ref=dst, send_sem=send, recv_sem=recv,
            device_id={"sector": device}, device_id_type=pl.DeviceIdType.MESH,
        )

    def seams(k):
        return [
            remote(
                state.at[k, d, :, depth if d == 0 else 1], seam_in.at[k, d],
                seam_send.at[k, d], seam_recv.at[k, d], partner,
            )
            for d in range(2)
        ]

    def sides(k, r):
        return [
            remote(
                radial_out.at[k, r, d], radial_in.at[k, r, d], radial_send.at[k, r, d],
                radial_recv.at[k, r, d], right if d == 0 else left,
            )
            for d in range(2)
        ]

    def rims(k):
        return [
            remote(
                rim_out.at[k, d], rim_in.at[k, d], rim_send.at[k, d], rim_recv.at[k, d],
                right if d == 0 else left,
            )
            for d in range(2)
        ]

    def circs(k, r):
        return remote(
            circ_out.at[k, r], circ_in.at[k, r], circ_send.at[k, r], circ_recv.at[k, r], partner
        )

    def corners(k):
        return remote(
            corner_out.at[k], corner_in.at[k], corner_send.at[k], corner_recv.at[k], partner
        )

    def send(sideways, across):
        for d, there in enumerate((has_right, has_left)):
            pl.when(there)(sideways[d].start)
        across.start()

    def arrive(sideways, across):
        for d, there in enumerate((has_left, has_right)):
            pl.when(there)(sideways[d].wait_recv)
        across.wait_recv()

    def sent(sideways, across):
        for d, there in enumerate((has_right, has_left)):
            pl.when(there)(sideways[d].wait_send)
        across.wait_send()

    def tables():
        wide = lax.broadcasted_iota(jnp.int32, (K, K), 0)
        pair = lax.broadcasted_iota(jnp.int32, (K, K), 1)
        for d in range(2):
            from_source = (source[d:d + 1, :] == wide).astype(jnp.float32).astype(jnp.bfloat16)
            to_target = jnp.where(
                (target[d:d + 1, :] == wide) & (pair < count[d]), 1.0, 0.0
            ).astype(jnp.bfloat16)
            moves = lax.dot_general(
                to_target, from_source, (((1,), (1,)), ((), ())),
                preferred_element_type=jnp.float32,
            ).astype(jnp.bfloat16)
            for part in range(2):
                for wave in range(2):
                    gather[d, part, :, wave * K:(wave + 1) * K] = jnp.dot(
                        inverse[sector, part, :, wave * K:(wave + 1) * K], moves,
                        preferred_element_type=jnp.float32,
                    ).astype(jnp.bfloat16)
            for v in range(VARS):
                for w in range(VARS):
                    total = right_char[v, d, 0] * left_char[0, d, w]
                    for c in range(1, VARS):
                        total = total + right_char[v, d, c] * left_char[c, d, w]
                    ghost_map[d, v * VARS + w] = total
                    for which, jac in enumerate((axial_jac, circ_jac)):
                        factors[which, d, v * VARS + w] = jnp.full(
                            (TILE, LANES), (-0.5 / diffusion) * jac[v, d, w], jnp.float32
                        )
        mode = lax.broadcasted_iota(jnp.int32, (K, LANES), 0)
        for s in range(4):
            angle = ((mode * offset[s]) & (NTH - 1)).astype(jnp.float32) * (2.0 * math.pi / NTH)
            phases[s, 0] = jnp.cos(angle)
            phases[s, 1] = jnp.sin(angle)

    def own_spectrum(k):
        both = jnp.concatenate(
            [
                packed([state[k, 0, v, depth] for v in range(VARS)]),
                packed([state[k, 1, v, 1] for v in range(VARS)]),
            ],
            axis=1,
        )
        spectrum[...] = dot3(forward[sector, 0], forward[sector, 1], both)

    def make_ghosts(k):
        both = jnp.concatenate(
            [packed([seam_in[k, d, v] for v in range(VARS)]) for d in range(2)], axis=1
        )
        whole = spectrum[...] + dot3(forward[1 - sector, 0], forward[1 - sector, 1], both)
        cosine, sine = phases[k, 0], phases[k, 1]
        for d in range(2):
            even = whole[:K, d * LANES:(d + 1) * LANES]
            odd = whole[K:, d * LANES:(d + 1) * LANES]
            turn = sine if d == 0 else -sine
            moved = jnp.concatenate([cosine * even - turn * odd, turn * even + cosine * odd], axis=0)
            raw = dot3(gather[d, 0], gather[d, 1], moved)
            planes = [unpacked(raw, w) for w in range(VARS)]
            for v in range(VARS):
                ghost = ghost_map[d, v * VARS] * planes[0]
                for w in range(1, VARS):
                    ghost = ghost + ghost_map[d, v * VARS + w] * planes[w]
                if d == 0:
                    state[k, 1, v, 0] = ghost
                else:
                    state[k, 0, v, depth + 1] = ghost

    def advance(k, r, a, last, edge):
        tiles = range(ROWS // TILE)
        if edge:
            up_row = corner_in[k, 2 * r:2 * r + 1, :]
            down_row = corner_in[k, 2 * r + 1:2 * r + 2, :]
        else:
            up_row = circ_in[k, r, 0, pl.ds(a, 1), :]
            down_row = circ_in[k, r, 1, pl.ds(a, 1), :]
        if not last:
            step = jnp.where(k == 2, diffusion * STATE_STEP[2], diffusion * STATE_STEP[0])
        new = [[None] * len(tiles) for _ in range(VARS)]
        for start in range(0, len(tiles), TOGETHER):
            chunk = range(start, start + TOGETHER)
            along, around, rate = {}, {}, {}
            for w in range(VARS):
                for t in chunk:
                    lo = t * TILE
                    here = pl.ds(lo, TILE)
                    x = state[k, r, w, a + 1, here]
                    before, after = state[k, r, w, a, here], state[k, r, w, a + 2, here]
                    if t == 0:
                        halo = turned(up_row, LANES - RADIAL - RADIAL * w)
                        up = jnp.where(row8 == 0, halo, turned(x, 1, 0))
                    else:
                        up = state[k, r, w, a + 1, pl.ds(lo - 1, TILE)]
                    if t == tiles[-1]:
                        halo = turned(down_row, -RADIAL * w)
                        down = jnp.where(row8 == TILE - 1, halo, turned(x, -1, 0))
                    else:
                        down = state[k, r, w, a + 1, pl.ds(lo + 1, TILE)]
                    previous = turned(jnp.where(at_last, up, x), RADIAL)
                    following = turned(jnp.where(at_first, down, x), -RADIAL)
                    if edge:
                        place = r * VARS + w
                        low = turned(rim_in[k, 0, here], -place)
                        high = turned(rim_in[k, 1, here], RADIAL - 1 - place)
                    else:
                        low = turned(radial_in[k, r, 0, w, here], -a)
                        high = turned(radial_in[k, r, 1, w, here], RADIAL - 1 - a)
                    inner = jnp.where(radial8 == 0, low, turned(x, 1))
                    outer = jnp.where(radial8 == RADIAL - 1, high, turned(x, -1))
                    along[w, t] = after - before
                    around[w, t] = following - previous
                    rate[w, t] = (
                        (after + before) + (following + previous) + (inner + outer) - 6.0 * x
                    )
            for v in range(VARS):
                for w in range(VARS):
                    one, two = factors[0, r, v * VARS + w], factors[1, r, v * VARS + w]
                    for t in chunk:
                        rate[v, t] = rate[v, t] + (one * along[w, t] + two * around[w, t])
                for t in chunk:
                    here = pl.ds(t * TILE, TILE)
                    base = state[0, r, v, a + 1, here]
                    if last:
                        total = state[1, r, v, a + 1, here] + 2.0 * state[2, r, v, a + 1, here]
                        total = total + state[3, r, v, a + 1, here] - base
                        out[r, v, a, here] = (
                            total * (1.0 / 3.0) + (diffusion * time_step / 6.0) * rate[v, t]
                        )
                    else:
                        n = base + step * rate[v, t]
                        state[k + 1, r, v, a + 1, here] = n
                        new[v][t] = n
                        if not edge:
                            mine = radial8 == a
                            radial_out[k + 1, r, 0, v, here] = jnp.where(
                                mine, turned(n, a - (RADIAL - 1)), radial_out[k + 1, r, 0, v, here]
                            )
                            radial_out[k + 1, r, 1, v, here] = jnp.where(
                                mine, turned(n, a), radial_out[k + 1, r, 1, v, here]
                            )
        if not last and not edge:
            pack_rows(k + 1, r, a, [n[0][:1] for n in new], [n[-1][TILE - 1:] for n in new])
        return new

    def stage(k, last=False):
        for r in range(2):
            arrive(sides(k, r), circs(k, r))

            def inside(a, carry):
                advance(k, r, a, last, False)
                return carry

            lax.fori_loop(r, depth - 1 + r, inside, 0)
            if not last:
                send(sides(k + 1, r), circs(k + 1, r))
        for copy in seams(k):
            copy.wait_recv()
        make_ghosts(k)
        arrive(rims(k), corners(k))
        for r in range(2):
            advance(k, r, (depth - 1) * (1 - r), last, True)
            if not last:
                seams(k + 1)[r].start()
        if not last:
            pack_edges(k + 1)
            send(rims(k + 1), corners(k + 1))
            own_spectrum(k + 1)

    for d, there in enumerate((has_left, has_right)):

        @pl.when(jnp.logical_not(there))
        def _():
            for k in range(4):
                rim_in[k, d] = jnp.zeros((ROWS, LANES), jnp.float32)
                for r in range(2):
                    radial_in[k, r, d] = jnp.zeros((VARS, ROWS, LANES), jnp.float32)

    for slot in range(4):
        for v in range(VARS):
            state[slot, 0, v, 0] = jnp.zeros((ROWS, LANES), jnp.float32)
            state[slot, 1, v, depth + 1] = jnp.zeros((ROWS, LANES), jnp.float32)

    loads[0].wait()
    loads[1].wait()
    pl.semaphore_wait(barrier, 3)
    for copy in seams(0):
        copy.start()
    for r in range(2):

        def take_in(a, carry):
            pack(0, r, a, [state[0, r, v, a + 1] for v in range(VARS)])
            return carry

        lax.fori_loop(r, depth - 1 + r, take_in, 0)
        send(sides(0, r), circs(0, r))
    pack_edges(0)
    send(rims(0), corners(0))
    for load in loads[2:]:
        load.wait()
    tables()
    own_spectrum(0)

    def early(k, carry):
        stage(k)
        return carry

    lax.fori_loop(0, 3, early, 0)
    stage(3, last=True)
    for k in range(4):
        for copy in seams(k):
            copy.wait_send()
        for r in range(2):
            sent(sides(k, r), circs(k, r))
        sent(rims(k), corners(k))


def fast_path(
    field, axial_jac, circ_jac, left_char, right_char, mode_source, mode_target, mode_count,
    section_offset,
):
    depth = field.shape[2]
    grid = field.reshape(2, VARS, depth, ROWS, LANES)
    forward, inverse = split_tables()
    plane = (ROWS, LANES)
    small = [jnp.transpose(m, (1, 0, 2)) for m in (axial_jac, circ_jac, left_char, right_char)]
    args = [
        grid, *small, mode_count, section_offset, mode_source, mode_target,
        jnp.asarray(forward), jnp.asarray(inverse),
    ]
    places = [pltpu.SMEM] * 6 + [pltpu.VMEM] * 4
    result = pl.pallas_call(
        step_kernel,
        out_shape=jax.ShapeDtypeStruct(grid.shape, jnp.float32),
        in_specs=[pl.BlockSpec(memory_space=pltpu.HBM)] * len(args),
        out_specs=pl.BlockSpec(memory_space=pltpu.VMEM),
        scratch_shapes=[place(x.shape, x.dtype) for place, x in zip(places, args[1:])] + [
            pltpu.VMEM((4, 2, VARS, depth + 2) + plane, jnp.float32),
            pltpu.VMEM((4, 2, VARS) + plane, jnp.float32),
            pltpu.VMEM((4, 2, 2, VARS) + plane, jnp.float32),
            pltpu.VMEM((4, 2, 2, VARS) + plane, jnp.float32),
            pltpu.VMEM((4, 2, 2, depth, LANES), jnp.float32),
            pltpu.VMEM((4, 2, 2, depth, LANES), jnp.float32),
            pltpu.VMEM((4, 2) + plane, jnp.float32),
            pltpu.VMEM((4, 2) + plane, jnp.float32),
            pltpu.VMEM((4, 8, LANES), jnp.float32),
            pltpu.VMEM((4, 8, LANES), jnp.float32),
            pltpu.VMEM((2, 2, HALF, 2 * K), jnp.bfloat16),
            pltpu.VMEM((4, 2, K, LANES), jnp.float32),
            pltpu.SMEM((2, VARS * VARS), jnp.float32),
            pltpu.VMEM((2 * K, 2 * LANES), jnp.float32),
            pltpu.VMEM((2, 2, VARS * VARS, TILE, LANES), jnp.float32),
            pltpu.SemaphoreType.DMA((len(args) + 1,)),
            pltpu.SemaphoreType.DMA((4, 2)),
            pltpu.SemaphoreType.DMA((4, 2)),
            pltpu.SemaphoreType.DMA((4, 2, 2)),
            pltpu.SemaphoreType.DMA((4, 2, 2)),
            pltpu.SemaphoreType.DMA((4, 2)),
            pltpu.SemaphoreType.DMA((4, 2)),
            pltpu.SemaphoreType.DMA((4, 2)),
            pltpu.SemaphoreType.DMA((4, 2)),
            pltpu.SemaphoreType.DMA((4,)),
            pltpu.SemaphoreType.DMA((4,)),
        ],
        compiler_params=pltpu.CompilerParams(
            collective_id=0, has_side_effects=True, vmem_limit_bytes=62 * 1024 * 1024
        ),
    )(*args)
    return result.reshape(field.shape)


def on_device(field, *rest):
    fits = lax.axis_size("sector") == 2 * NB and field.shape[4] == ROWS * LANES
    return (fast_path if fits else general_path)(field, *rest)


def solution(mesh):
    in_specs = (P("group", None, None, "sector", None), P(), P(), P(), P(), P(), P(), P(), P())
    out_specs = P("group", None, None, "sector", None)
    return jax.shard_map(
        on_device, mesh=mesh, in_specs=in_specs, out_specs=out_specs, check_vma=False
    )
```
